512 devices in a mesh: dp: 16 (over y, core), tensor: 8 (over z), adapter: 4 (over x).
Axes of the slice: x: 4, y: 8, z: 8, core: 2. Of those that a mesh axis runs over, the one named last changes fastest.
Arguments:
- queries: bfloat16 [4096, 8, 4, 128], P(('dp', 'tensor'), None, 'adapter'), may hold values from -125 to 125
- key_cache_rows: bfloat16 [4096, 16, 4, 128], P(('dp', 'tensor'), None, 'adapter'), may hold values from -6.5 to 6.5
- value_cache_rows: bfloat16 [4096, 16, 4, 128], P(('dp', 'tensor'), None, 'adapter'), may hold values from -6 to 6
- row_cache_length: int32 [4096], P(('dp', 'tensor')), may hold values from 2 to 16, as said below
- row_adapter_index: int32 [4096], P(('dp', 'tensor')), may hold values from 0 to 255, as said below
- adapter_storage_slot: int32 [256], replicated, may hold values from 0 to 255, as said below
- output_projection_weight: bfloat16 [8, 4, 128, 8192], P(None, 'adapter', None, 'tensor'), may hold values from -0.09375 to 0.09375
- adapter_down_weight: bfloat16 [256, 64, 8, 4, 128], P(('dp', 'tensor'), None, None, 'adapter'), may hold values from -0.09375 to 0.09375
- adapter_up_weight: bfloat16 [256, 64, 8, 1024], P(('dp', 'tensor'), None, None, 'adapter'), may hold values from -0.75 to 0.75
Outputs:
- mixed_out: bfloat16 [4096, 8192], P('dp', ('tensor', 'adapter'))
The draws below stay inside these ranges and needn't reach their ends.
Inputs may be any that keep to these rules, and one draw needn't show every extreme that they name: `adapter_storage_slot`: a permutation; slot s lies with owner s // 2 (the index along dp+tensor) as its adapter s % 2. `row_adapter_index`: in the 32 rows of one device (aligned blocks) at most 2 rows name adapters of one owner; one owner, the same for every device, gets exactly 2 rows of every device. `row_cache_length`: 16 is reached in the rows of every device.
All inputs are finite; a program needn't handle non-finite values.
Results may differ from the reference program's by a relative error of at most 0.0064.
Values may be sent and summed in bfloat16 or wider, within the bound.
A program may use at most 64 MiB of HBM per device.

```python
import jax
import jax.numpy as jnp
from jax import lax

MODEL_WIDTH = 8192
QUERY_PER_KEY = 8
KEY_VALUE_HEADS = 4
HEAD_WIDTH = 128
ADAPTER_RANK = 64
ADAPT_DEV = 2
ROW_DEV = 256
CACHE = 16
DECODE_ROWS = 4096
SEND = 32
OWNERS = 128
ADAPTER_COUNT = 256
CAP = 2
TENSOR_COLUMNS = 1024
N_TENSOR = 8


def shared_slots(key):
    return jax.random.permutation(key, ADAPTER_COUNT).astype(jnp.int32)


def shared_keys(key):
    fresh = jax.random.normal(jax.random.fold_in(key, 101), (DECODE_ROWS, CACHE, KEY_VALUE_HEADS, HEAD_WIDTH), jnp.float32)
    return jnp.clip(fresh, -6.0, 6.0)


def draw_adapter_storage_slot(key, part):
    return shared_slots(key)


def draw_row_adapter_index(key, part):
    slot_table = shared_slots(key)
    key = jax.random.fold_in(key, 2)
    holder = jnp.argsort(slot_table).astype(jnp.int32)
    blocks = DECODE_ROWS // SEND
    key_hot, key_pool, key_pick = jax.random.split(key, 3)
    hottest = jax.random.randint(key_hot, (), 0, OWNERS).astype(jnp.int32)

    def one_block(block_key):
        pool_key, order_key = jax.random.split(block_key)
        pooled = (jax.random.permutation(pool_key, (OWNERS - 1) * CAP)[:SEND - CAP] // CAP).astype(jnp.int32)
        others = pooled + (pooled >= hottest).astype(jnp.int32)
        owners_all = jnp.concatenate([jnp.full((CAP,), 1, jnp.int32) * hottest, others])
        return owners_all[jax.random.permutation(order_key, SEND)]
    owner_rows = jax.vmap(one_block)(jax.random.split(key_pool, blocks))
    within = jax.random.randint(key_pick, (blocks, SEND), 0, ADAPT_DEV).astype(jnp.int32)
    slot_rows = owner_rows * ADAPT_DEV + within
    return holder[slot_rows.reshape(DECODE_ROWS)].astype(jnp.int32)


def draw_row_cache_length(key, part):
    key = jax.random.fold_in(key, 3)
    key_len, key_pos = jax.random.split(key)
    blocks = DECODE_ROWS // SEND
    lengths_all = jax.random.randint(key_len, (blocks, SEND), 2, CACHE + 1).astype(jnp.int32)
    longest = jax.random.randint(key_pos, (blocks, 1), 0, SEND).astype(jnp.int32)
    filled = jnp.where(jnp.arange(SEND, dtype=jnp.int32)[None, :] == longest, CACHE, lengths_all)
    return filled.reshape(DECODE_ROWS).astype(jnp.int32)


def draw_key_cache_rows(key, part):
    base_keys = shared_keys(key)
    return base_keys.astype(jnp.bfloat16)


def draw_queries(key, part):
    key = jax.random.fold_in(key, 5)
    fresh = jnp.clip(jax.random.normal(key, (DECODE_ROWS, QUERY_PER_KEY, KEY_VALUE_HEADS, HEAD_WIDTH), jnp.float32), -6.0, 6.0)
    return fresh.astype(jnp.bfloat16)


def level_of(stream_key, extent, cuts, smallest, largest):
    gain, own = 1.0, jax.random.fold_in(stream_key, 6)
    for axis_at, blocks in cuts:
        draws = jnp.exp(jax.random.uniform(jax.random.fold_in(own, axis_at), (blocks,), jnp.float32, smallest / len(cuts), largest / len(cuts)))
        gain = gain * jnp.repeat(draws, extent[axis_at] // blocks).reshape([-1 if axis == axis_at else 1 for axis in range(len(extent))])
    return gain


def gaussian(key, dims, scale, limit, cuts=(), kind=jnp.bfloat16):
    values = jax.random.normal(key, dims, jnp.float32) * scale
    if len(cuts) > 0:
        values = level_of(key, dims, cuts, -0.22, 0.18) * values
    return jnp.clip(values, min=-limit, max=limit).astype(kind)


def setup_inputs(seed: int = 0) -> dict:
    arg_keys = jax.random.split(jax.random.key(seed), 10)
    queries = draw_queries(jax.random.fold_in(arg_keys[9], 71), 0)
    key_cache_rows = draw_key_cache_rows(jax.random.fold_in(arg_keys[9], 71), 0)
    value_cache_rows = gaussian(arg_keys[2], (DECODE_ROWS, CACHE, KEY_VALUE_HEADS, HEAD_WIDTH), 1.0, 6.0, ((0, 128), (2, 4)))
    row_cache_length = draw_row_cache_length(jax.random.fold_in(arg_keys[9], 71), 0)
    row_adapter_index = draw_row_adapter_index(jax.random.fold_in(arg_keys[9], 71), 0)
    adapter_storage_slot = draw_adapter_storage_slot(jax.random.fold_in(arg_keys[9], 71), 0)
    output_projection_weight = gaussian(arg_keys[6], (QUERY_PER_KEY, KEY_VALUE_HEADS, HEAD_WIDTH, MODEL_WIDTH), (QUERY_PER_KEY * KEY_VALUE_HEADS * HEAD_WIDTH) ** -0.5, 0.09375, ((1, 4), (3, 8)))
    adapter_down_weight = gaussian(arg_keys[7], (ADAPTER_COUNT, ADAPTER_RANK, QUERY_PER_KEY, KEY_VALUE_HEADS, HEAD_WIDTH), (QUERY_PER_KEY * KEY_VALUE_HEADS * HEAD_WIDTH) ** -0.5, 0.09375, ((0, 128), (3, 4)))
    adapter_up_weight = gaussian(arg_keys[8], (ADAPTER_COUNT, ADAPTER_RANK, N_TENSOR, TENSOR_COLUMNS), ADAPTER_RANK ** -0.5, 0.75, ((0, 128), (3, 4)))
    return dict(queries=queries, key_cache_rows=key_cache_rows, value_cache_rows=value_cache_rows, row_cache_length=row_cache_length, row_adapter_index=row_adapter_index, adapter_storage_slot=adapter_storage_slot, output_projection_weight=output_projection_weight, adapter_down_weight=adapter_down_weight, adapter_up_weight=adapter_up_weight)


def attend_block(kernel_operands):
    query_rows, key_rows, value_rows, length_rows = kernel_operands
    scores = jnp.einsum("rgkd,rckd->rgkc", query_rows.astype(jnp.float32), key_rows.astype(jnp.float32)) * (HEAD_WIDTH ** -0.5)
    in_cache = jnp.arange(CACHE, dtype=jnp.int32)[None, None, None, :] < length_rows[:, None, None, None]
    scores = jnp.where(in_cache, scores, -1e30)
    row_max = jnp.max(scores, axis=-1, keepdims=True)
    weights = jnp.exp(scores - row_max)
    weights = (weights / jnp.sum(weights, axis=-1, keepdims=True)).astype(jnp.bfloat16)
    weights = lax.optimization_barrier(weights)
    attention_output = jnp.einsum("rgkc,rckd->rgkd", weights.astype(jnp.float32), value_rows.astype(jnp.float32))
    return attention_output.astype(jnp.bfloat16)


def reference(queries, key_cache_rows, value_cache_rows, row_cache_length, row_adapter_index, adapter_storage_slot, output_projection_weight, adapter_down_weight, adapter_up_weight):
    blocks = DECODE_ROWS // ROW_DEV
    attention_output = lax.map(attend_block, (
        queries.reshape(blocks, ROW_DEV, QUERY_PER_KEY, KEY_VALUE_HEADS, HEAD_WIDTH),
        key_cache_rows.reshape(blocks, ROW_DEV, CACHE, KEY_VALUE_HEADS, HEAD_WIDTH),
        value_cache_rows.reshape(blocks, ROW_DEV, CACHE, KEY_VALUE_HEADS, HEAD_WIDTH),
        row_cache_length.reshape(blocks, ROW_DEV)))
    input_width = QUERY_PER_KEY * KEY_VALUE_HEADS * HEAD_WIDTH
    attention_output = attention_output.reshape(DECODE_ROWS, input_width)
    plain_projection = jnp.dot(attention_output, output_projection_weight.reshape(input_width, MODEL_WIDTH), preferred_element_type=jnp.float32)
    slot_lookup = adapter_storage_slot[row_adapter_index].astype(jnp.int32)
    gathered_down_maps = adapter_down_weight.reshape(ADAPTER_COUNT, ADAPTER_RANK, input_width)
    gathered_up_maps = adapter_up_weight.reshape(ADAPTER_COUNT, ADAPTER_RANK, MODEL_WIDTH)

    def adapter_block(kernel_operands):
        rows_in, slots_in = kernel_operands
        shrunk = jnp.einsum("rf,rkf->rk", rows_in.astype(jnp.float32), gathered_down_maps[slots_in].astype(jnp.float32))
        reduced = lax.optimization_barrier(shrunk.astype(jnp.bfloat16))
        grown = jnp.einsum("rk,rkd->rd", reduced.astype(jnp.float32), gathered_up_maps[slots_in].astype(jnp.float32))
        return grown.astype(jnp.bfloat16)

    adapter_delta = lax.map(adapter_block, (attention_output.reshape(DECODE_ROWS // 16, 16, input_width), slot_lookup.reshape(DECODE_ROWS // 16, 16)))
    adapter_delta = adapter_delta.reshape(DECODE_ROWS, MODEL_WIDTH)
    return (plain_projection + adapter_delta.astype(jnp.float32)).astype(jnp.bfloat16)
```

```python
import functools

import jax
import jax.numpy as jnp
from jax import lax
from jax.experimental import pallas as pl
from jax.experimental.pallas import tpu as pltpu
from jax.sharding import PartitionSpec as P

MESH = pl.DeviceIdType.MESH
CAP = 2
F32 = jnp.float32
BF16 = jnp.bfloat16


def iota(shape, dim):
    return lax.broadcasted_iota(jnp.int32, shape, dim)


def dot(a, b):
    return jnp.dot(a, b, preferred_element_type=F32)


def dot_t(a, b):
    return lax.dot_general(a, b, (((1,), (1,)), ((), ())), preferred_element_type=F32)


def regroup(rows, groups):
    n = rows * groups
    out, into = iota((n, n), 0), iota((n, n), 1)
    return jnp.where(into == (out % rows) * groups + out // rows, 1.0, 0.0).astype(BF16)


def column_of(row, n):
    return jnp.sum(jnp.where(iota((n, n), 0) == iota((n, n), 1), row, 0.0), axis=1, keepdims=True)


def row_of(column, n):
    return jnp.sum(jnp.where(iota((n, n), 0) == iota((n, n), 1), column, 0.0), axis=0, keepdims=True)


def attend(q_ref, k_ref, v_ref, length_row, rows, groups, cache):
    per = 128 // cache if rows * cache > 128 else rows
    width = per * cache
    lengths = jnp.sum(
        jnp.where(iota((rows * groups, rows), 0) // groups == iota((rows * groups, rows), 1), length_row, 0.0),
        axis=1,
        keepdims=True,
    )
    outs = []
    for first in range(0, rows, per):
        q = q_ref[first * groups : (first + per) * groups, :]
        k = k_ref[first * cache : (first + per) * cache, :]
        v = v_ref[first * cache : (first + per) * cache, :]
        shape = (per * groups, width)
        lane = iota(shape, 1)
        live = (iota(shape, 0) // groups == lane // cache) & (
            (lane % cache).astype(F32) < lengths[first * groups : (first + per) * groups, :]
        )
        scores = jnp.where(live, dot_t(q, k) * (q.shape[-1] ** -0.5), -1e30)
        weights = jnp.exp(scores - jnp.max(scores, axis=1, keepdims=True))
        weights = jnp.where(live, weights, 0.0)
        weights = (weights / jnp.sum(weights, axis=1, keepdims=True)).astype(BF16)
        outs.append(dot(weights, v).astype(BF16))
    return jnp.concatenate(outs, axis=0)


def kernel(
    nd, nt, na, groups, cache, holding,
    q_ref, k_ref, v_ref, len_ref, idx_ref, slot_ref, w_hbm, down_ref, up_ref, out_ref,
    xg, pk, rx, w_ref, downp, upp, upg, btx, brx, acc, ptx, prx, redg, ret_tx, ret_rx,
    w_sem, z_send, z_recv, u_send, u_recv, y_send, y_recv, b_send, b_recv, p_send, p_recv,
    r_send, r_recv, f_send, f_recv,
):
    d, t, a = lax.axis_index("dp"), lax.axis_index("tensor"), lax.axis_index("adapter")
    rows = q_ref.shape[0] // groups
    feat = groups * 128
    spots = nt * CAP
    slots = nd * spots
    rank2 = 128
    all_rows = nt * rows
    cols = acc.shape[1]

    def z_dev(k):
        return (d, lax.rem(t + k, nt), a)

    def y_dev(k):
        return (lax.rem(d + k, nd), t, a)

    def x_dev(k):
        return (d, t, lax.rem(a + k, na))

    w_copy = pltpu.make_async_copy(w_hbm, w_ref, w_sem)
    w_copy.start()
    barrier = pltpu.get_barrier_semaphore()
    for n, dev in ((nt, z_dev), (nd, y_dev), (na, x_dev)):
        def greet(k, c, dev=dev):
            pl.semaphore_signal(barrier, inc=1, device_id=dev(k), device_id_type=MESH)
            return c
        lax.fori_loop(1, n, greet, 0)

    idx_col = column_of(idx_ref[...].astype(F32), rows)
    table = slot_ref.shape[1]
    slot_col = jnp.sum(
        jnp.where(idx_col == iota((rows, table), 1).astype(F32), slot_ref[...].astype(F32), 0.0),
        axis=1, keepdims=True,
    )
    owner_col = jnp.floor(slot_col * (1.0 / holding))
    local_col = slot_col - holding * owner_col
    owner_row = row_of(owner_col, rows)
    earlier = (owner_row == owner_col) & (iota((rows, rows), 1) < iota((rows, rows), 0))
    pos_col = jnp.sum(jnp.where(earlier, 1.0, 0.0), axis=1, keepdims=True)
    code = owner_col * CAP + pos_col + 1.0
    tags = jnp.where((iota((rows, rank2), 1) // (rank2 // holding)).astype(F32) == local_col, code, 0.0)

    att = attend(q_ref, k_ref, v_ref, len_ref[...].astype(F32), rows, groups, cache)
    swap = regroup(rows, groups)
    att = dot(swap, att).astype(BF16)
    mine = pl.ds(pl.multiple_of(t * rows, rows), rows)
    for g in range(groups):
        xg[mine, g * 128 : (g + 1) * 128] = att[g * rows : (g + 1) * rows, :]
    xg[mine, feat : feat + rank2] = tags.astype(BF16)

    pl.semaphore_wait(barrier, (nt - 1) + (nd - 1) + (na - 1))

    def z_copy(k, block):
        part = xg.at[pl.ds(pl.multiple_of(block * rows, rows), rows)]
        return pltpu.make_async_remote_copy(
            src_ref=part, dst_ref=part, send_sem=z_send.at[k], recv_sem=z_recv.at[k],
            device_id=z_dev(k), device_id_type=MESH)

    def z_start(k, c):
        z_copy(k, t).start()
        return c
    lax.fori_loop(1, nt, z_start, 0)

    step = 256 // groups
    swap_w = regroup(step, groups)
    for b in range(holding * 64 // step):
        part = slice(b * step * groups, (b + 1) * step * groups)
        up = dot(swap_w, up_ref[part, :]).astype(BF16)
        for g in range(nt):
            upp[g, b * step : (b + 1) * step, :] = up[g * step : (g + 1) * step, :]

    def u_copy(k):
        return pltpu.make_async_remote_copy(
            src_ref=upp.at[lax.rem(t + k, nt)], dst_ref=upg.at[t], send_sem=u_send.at[k],
            recv_sem=u_recv.at[k], device_id=z_dev(k), device_id_type=MESH)

    def u_start(k, c):
        u_copy(k).start()
        return c
    lax.fori_loop(1, nt, u_start, 0)
    upg[t] = upp[t]
    for b in range(holding * 64 // step):
        part = slice(b * step * groups, (b + 1) * step * groups)
        down = dot(swap_w, down_ref[part, :]).astype(BF16)
        for g in range(groups):
            downp[b * step : (b + 1) * step, g * 128 : (g + 1) * 128] = down[g * step : (g + 1) * step, :]

    def z_wait(k, c):
        z_copy(k, lax.rem(t - k + nt, nt)).wait_recv()
        return c
    lax.fori_loop(1, nt, z_wait, 0)

    tag = xg[:, feat : feat + rank2].astype(F32)
    codes = tag[:, 0:1] + tag[:, rank2 // 2 : rank2 // 2 + 1] - 1.0
    owners = jnp.floor(codes * (1.0 / CAP))
    pos = codes - CAP * owners
    owner_d = jnp.floor(owners * (1.0 / nt))
    owner_t = owners - nt * owner_d
    place = (iota((all_rows, 1), 0) // rows).astype(F32) * CAP + pos
    target = jnp.where(owner_t == t.astype(F32), owner_d * spots + place, -1.0)
    target_row = row_of(target, all_rows)
    route = jnp.where(iota((slots, all_rows), 0).astype(F32) == target_row, 1.0, 0.0).astype(BF16)
    pk[...] = dot(route, xg[...]).astype(BF16)

    def spot(block):
        return pl.ds(pl.multiple_of(block * spots, spots), spots)

    def y_copy(k):
        return pltpu.make_async_remote_copy(
            src_ref=pk.at[spot(lax.rem(d + k, nd))], dst_ref=rx.at[spot(d)], send_sem=y_send.at[k],
            recv_sem=y_recv.at[k], device_id=y_dev(k), device_id_type=MESH)

    def y_start(k, c):
        y_copy(k).start()
        return c
    lax.fori_loop(1, nd, y_start, 0)
    rx[spot(d), :] = pk[spot(d), :]

    w_copy.wait()
    x = xg[:, :feat]

    def b_copy(k):
        return pltpu.make_async_remote_copy(
            src_ref=btx.at[k], dst_ref=brx.at[k], send_sem=b_send.at[k],
            recv_sem=b_recv.at[k], device_id=x_dev(k), device_id_type=MESH)
    for k in range(1, na):
        part = pl.ds(pl.multiple_of(lax.rem(a + k, na) * cols, cols), cols)
        btx[k] = dot(x, w_ref[:, part]).astype(BF16)
        b_copy(k).start()
    acc[...] = dot(x, w_ref[:, pl.ds(pl.multiple_of(a * cols, cols), cols)])

    def y_wait(k, c):
        y_copy(k).wait_recv()
        return c
    lax.fori_loop(1, nd, y_wait, 0)

    shrunk = dot_t(rx[:, :feat], downp[...])
    shrunk = jnp.where(rx[:, feat : feat + rank2].astype(F32) > 0.0, shrunk, 0.0)
    ptx[...] = shrunk.astype(BF16)

    def p_copy(k):
        return pltpu.make_async_remote_copy(
            src_ref=ptx, dst_ref=prx.at[k], send_sem=p_send.at[k],
            recv_sem=p_recv.at[k], device_id=x_dev(k), device_id_type=MESH)
    for k in range(1, na):
        p_copy(k).start()
    for k in range(1, na):
        p_copy(k).wait_recv()
        shrunk = shrunk + prx[k].astype(F32)
    redg[t] = shrunk.astype(BF16)

    def r_copy(k):
        return pltpu.make_async_remote_copy(
            src_ref=redg.at[t], dst_ref=redg.at[t], send_sem=r_send.at[k],
            recv_sem=r_recv.at[k], device_id=z_dev(k), device_id_type=MESH)

    def r_start(k, c):
        r_copy(k).start()
        return c
    lax.fori_loop(1, nt, r_start, 0)

    def r_wait(k, c):
        r_copy(k).wait_recv()
        u_copy(k).wait_recv()
        return c
    lax.fori_loop(1, nt, r_wait, 0)
    for g in range(nt):
        grown = dot(redg[g], upg[g]).astype(BF16)
        ret_tx[:, g, :, :] = grown.reshape(nd, spots, cols)

    def f_copy(k):
        return pltpu.make_async_remote_copy(
            src_ref=ret_tx.at[lax.rem(d + k, nd)], dst_ref=ret_rx.at[d], send_sem=f_send.at[k],
            recv_sem=f_recv.at[k], device_id=y_dev(k), device_id_type=MESH)

    def f_start(k, c):
        f_copy(k).start()
        return c
    lax.fori_loop(1, nd, f_start, 0)
    ret_rx[d] = ret_tx[d]

    for k in range(1, na):
        b_copy(k).wait_recv()
        acc[...] += brx[k].astype(F32)
    target = owners * spots + place

    def f_wait(k, c):
        f_copy(k).wait_recv()
        return c
    lax.fori_loop(1, nd, f_wait, 0)
    total = acc[...]
    span = nt * spots
    for g in range(nd):
        pick = jnp.where((iota((all_rows, span), 1) + g * span).astype(F32) == target, 1.0, 0.0).astype(BF16)
        total = total + dot(pick, ret_rx[g].reshape(span, cols))
    out_ref[...] = total.astype(BF16)

    def drain_z(k, c):
        z_copy(k, t).wait_send()
        u_copy(k).wait_send()
        r_copy(k).wait_send()
        return c
    lax.fori_loop(1, nt, drain_z, 0)

    def drain_y(k, c):
        y_copy(k).wait_send()
        f_copy(k).wait_send()
        return c
    lax.fori_loop(1, nd, drain_y, 0)
    for k in range(1, na):
        b_copy(k).wait_send()
        p_copy(k).wait_send()


def body(sizes, q, kc, vc, lengths, index, table, w, down, up):
    nd, nt, na = sizes
    rows, groups, _, width = q.shape
    cache = kc.shape[1]
    holding, rank = down.shape[0], down.shape[1]
    feat = groups * width
    columns = w.shape[-1]
    cols = columns // na
    spots = nt * CAP
    slots = nd * spots
    wide = feat + holding * rank
    hr = holding * rank
    vmem = pl.BlockSpec(memory_space=pltpu.VMEM)
    dma = pltpu.SemaphoreType.DMA
    return pl.pallas_call(
        functools.partial(kernel, nd, nt, na, groups, cache, holding),
        out_shape=jax.ShapeDtypeStruct((nt * rows, cols), BF16),
        in_specs=[vmem] * 6 + [pl.BlockSpec(memory_space=pl.ANY)] + [vmem] * 2,
        out_specs=vmem,
        scratch_shapes=[
            pltpu.VMEM((nt * rows, wide), BF16),
            pltpu.VMEM((slots, wide), BF16),
            pltpu.VMEM((slots, wide), BF16),
            pltpu.VMEM((feat, columns), BF16),
            pltpu.VMEM((hr, feat), BF16),
            pltpu.VMEM((nt, hr, cols), BF16),
            pltpu.VMEM((nt, hr, cols), BF16),
            pltpu.VMEM((na, nt * rows, cols), BF16),
            pltpu.VMEM((na, nt * rows, cols), BF16),
            pltpu.VMEM((nt * rows, cols), F32),
            pltpu.VMEM((slots, hr), BF16),
            pltpu.VMEM((na, slots, hr), BF16),
            pltpu.VMEM((nt, slots, hr), BF16),
            pltpu.VMEM((nd, nt, spots, cols), BF16),
            pltpu.VMEM((nd, nt, spots, cols), BF16),
            dma,
            dma((nt,)), dma((nt,)), dma((nt,)), dma((nt,)),
            dma((nd,)), dma((nd,)),
            dma((na,)), dma((na,)), dma((na,)), dma((na,)),
            dma((nt,)), dma((nt,)),
            dma((nd,)), dma((nd,)),
        ],
        compiler_params=pltpu.CompilerParams(
            collective_id=0, has_side_effects=True, vmem_limit_bytes=40 * 1024 * 1024
        ),
    )(
        q.reshape(rows * groups, width),
        kc.reshape(rows * cache, width),
        vc.reshape(rows * cache, width),
        lengths.reshape(1, rows),
        index.reshape(1, rows),
        table.reshape(1, -1),
        w.reshape(feat, columns),
        down.reshape(hr * groups, width),
        up.reshape(hr * nt, cols),
    )


def solution(mesh):
    sizes = tuple(mesh.shape[name] for name in ("dp", "tensor", "adapter"))
    return jax.shard_map(
        functools.partial(body, sizes),
        mesh=mesh,
        in_specs=(
            P(("dp", "tensor"), None, "adapter", None),
            P(("dp", "tensor"), None, "adapter", None),
            P(("dp", "tensor"), None, "adapter", None),
            P(("dp", "tensor")),
            P(("dp", "tensor")),
            P(),
            P(None, "adapter", None, "tensor"),
            P(("dp", "tensor"), None, None, "adapter", None),
            P(("dp", "tensor"), None, None, "adapter"),
        ),
        out_specs=P("dp", ("tensor", "adapter")),
        check_vma=False,
    )
```

```python
import functools

import jax
import jax.numpy as jnp
from jax import lax
from jax.experimental import pallas as pl
from jax.experimental.pallas import tpu as pltpu
from jax.sharding import PartitionSpec as P

MESH = pl.DeviceIdType.MESH
CAP = 2
F32 = jnp.float32
BF16 = jnp.bfloat16


def iota(shape, dim):
    return lax.broadcasted_iota(jnp.int32, shape, dim)


def dot(a, b):
    return jnp.dot(a, b, preferred_element_type=F32)


def dot_t(a, b):
    return lax.dot_general(a, b, (((1,), (1,)), ((), ())), preferred_element_type=F32)


def regroup(rows, groups):
    n = rows * groups
    out, into = iota((n, n), 0), iota((n, n), 1)
    return jnp.where(into == (out % rows) * groups + out // rows, 1.0, 0.0).astype(BF16)


def column_of(row, n):
    return jnp.sum(jnp.where(iota((n, n), 0) == iota((n, n), 1), row, 0.0), axis=1, keepdims=True)


def row_of(column, n):
    return jnp.sum(jnp.where(iota((n, n), 0) == iota((n, n), 1), column, 0.0), axis=0, keepdims=True)


def attend(q_ref, k_ref, v_ref, length_row, rows, groups, cache):
    per = 128 // cache if rows * cache > 128 else rows
    width = per * cache
    lengths = jnp.sum(
        jnp.where(iota((rows * groups, rows), 0) // groups == iota((rows * groups, rows), 1), length_row, 0.0),
        axis=1,
        keepdims=True,
    )
    outs = []
    for first in range(0, rows, per):
        q = q_ref[first * groups : (first + per) * groups, :]
        k = k_ref[first * cache : (first + per) * cache, :]
        v = v_ref[first * cache : (first + per) * cache, :]
        shape = (per * groups, width)
        lane = iota(shape, 1)
        live = (iota(shape, 0) // groups == lane // cache) & (
            (lane % cache).astype(F32) < lengths[first * groups : (first + per) * groups, :]
        )
        scores = jnp.where(live, dot_t(q, k) * (q.shape[-1] ** -0.5), -1e30)
        weights = jnp.exp(scores - jnp.max(scores, axis=1, keepdims=True))
        weights = jnp.where(live, weights, 0.0)
        weights = (weights / jnp.sum(weights, axis=1, keepdims=True)).astype(BF16)
        outs.append(dot(weights, v).astype(BF16))
    return jnp.concatenate(outs, axis=0)


def order_of(chips):
    near = [0]
    for j in range(1, chips // 2 + 1):
        near += [j] if 2 * j == chips else [j, chips - j]
    cuts = sorted({0, min(3, chips), min(5, chips), chips})
    return near, [(2 * lo, 2 * hi) for lo, hi in zip(cuts[:-1], cuts[1:])]


def kernel(
    nd, nt, na, groups, cache, holding,
    q_hbm, k_hbm, v_hbm, len_hbm, idx_hbm, slot_hbm, w_hbm, down_hbm, up_hbm, out_ref,
    q_ref, k_ref, v_ref, len_ref, idx_ref, slot_ref, down_ref, up_ref,
    xg, pk, rx, w_ref, downp, upp, upg, btx, brx, acc, ptx, prx, redg, ret_tx, ret_rx,
    in_sem, z_send, z_recv, u_send, u_recv, y_send, y_recv, b_send, b_recv, p_send, p_recv,
    r_send, r_recv, f_send, f_recv,
):
    d, t, a = lax.axis_index("dp"), lax.axis_index("tensor"), lax.axis_index("adapter")
    rows = q_ref.shape[0] // groups
    feat = groups * 128
    spots = nt * CAP
    slots = nd * spots
    half = 64
    lanes = 2 * half
    all_rows = nt * rows
    cols = acc.shape[1]
    chips = nd // 2
    near, runs = order_of(chips)
    chip, core = d // 2, d % 2

    def dp_at(m):
        return 2 * lax.rem(chip + near[m // 2], chips) + lax.rem(core + m % 2, 2)

    def back(m):
        return 2 * near.index((chips - near[m // 2]) % chips) + m % 2

    def z_dev(k):
        return (d, lax.rem(t + k, nt), a)

    def x_dev(k):
        return (d, t, lax.rem(a + k, na))

    fetches = [
        pltpu.make_async_copy(src, dst, in_sem.at[n])
        for n, (src, dst) in enumerate((
            (idx_hbm, idx_ref), (slot_hbm, slot_ref), (len_hbm, len_ref), (q_hbm, q_ref), (k_hbm, k_ref),
            (v_hbm, v_ref), (up_hbm, up_ref), (down_hbm, down_ref), (w_hbm, w_ref)))
    ]
    for fetch in fetches:
        fetch.start()
    barrier = pltpu.get_barrier_semaphore()

    def greet_z(k, c):
        pl.semaphore_signal(barrier, inc=1, device_id=z_dev(k), device_id_type=MESH)
        return c

    def greet_y(k, c):
        pl.semaphore_signal(barrier, inc=1, device_id=(lax.rem(d + k, nd), t, a), device_id_type=MESH)
        return c

    def greet_x(k, c):
        pl.semaphore_signal(barrier, inc=1, device_id=x_dev(k), device_id_type=MESH)
        return c
    lax.fori_loop(1, nt, greet_z, 0)
    lax.fori_loop(1, nd, greet_y, 0)
    lax.fori_loop(1, na, greet_x, 0)

    for fetch in fetches[:6]:
        fetch.wait()
    idx_col = column_of(idx_ref[...].astype(F32), rows)
    table = slot_ref.shape[1]
    slot_col = jnp.sum(
        jnp.where(idx_col == iota((rows, table), 1).astype(F32), slot_ref[...].astype(F32), 0.0),
        axis=1, keepdims=True,
    )
    owner_col = jnp.floor(slot_col * (1.0 / holding))
    local_col = slot_col - holding * owner_col
    owner_row = row_of(owner_col, rows)
    earlier = (owner_row == owner_col) & (iota((rows, rows), 1) < iota((rows, rows), 0))
    pos_col = jnp.sum(jnp.where(earlier, 1.0, 0.0), axis=1, keepdims=True)
    lane = iota((rows, lanes), 1)
    tags = jnp.where(lane == 0, owner_col * CAP + pos_col, jnp.where(lane == 1, local_col, 0.0))

    att = attend(q_ref, k_ref, v_ref, len_ref[...].astype(F32), rows, groups, cache)
    swap = regroup(rows, groups)
    att = dot(swap, att).astype(BF16)
    mine = pl.ds(pl.multiple_of(t * rows, rows), rows)
    for g in range(groups):
        xg[mine, g * 128 : (g + 1) * 128] = att[g * rows : (g + 1) * rows, :]
    xg[mine, feat : feat + lanes] = tags.astype(BF16)

    pl.semaphore_wait(barrier, (nt - 1) + (nd - 1) + (na - 1))

    def z_copy(k, block):
        part = xg.at[pl.ds(pl.multiple_of(block * rows, rows), rows)]
        return pltpu.make_async_remote_copy(
            src_ref=part, dst_ref=part, send_sem=z_send.at[k], recv_sem=z_recv.at[k],
            device_id=z_dev(k), device_id_type=MESH)

    def z_start(k, c):
        z_copy(k, t).start()
        return c
    lax.fori_loop(1, nt, z_start, 0)

    fetches[6].wait()
    fetches[7].wait()
    step = 256 // groups
    swap_w = regroup(step, groups)
    for b in range(holding * half // step):
        part = slice(b * step * groups, (b + 1) * step * groups)
        up = dot(swap_w, up_ref[part, :]).astype(BF16)
        for g in range(nt):
            upp[g, b * step : (b + 1) * step, :] = up[g * step : (g + 1) * step, :]
        down = dot(swap_w, down_ref[part, :]).astype(BF16)
        for g in range(groups):
            downp[b * step : (b + 1) * step, g * 128 : (g + 1) * 128] = down[g * step : (g + 1) * step, :]
    upg[t] = upp[t]

    def z_wait(k, c):
        z_copy(k, lax.rem(t - k + nt, nt)).wait_recv()
        return c
    lax.fori_loop(1, nt, z_wait, 0)

    tag = xg[:, feat : feat + lanes].astype(F32)
    codes, local = tag[:, 0:1], tag[:, 1:2]
    owners = jnp.floor(codes * (1.0 / CAP))
    pos = codes - CAP * owners
    owner_d = jnp.floor(owners * (1.0 / nt))
    owner_t = owners - nt * owner_d
    place = (iota((all_rows, 1), 0) // rows).astype(F32) * CAP + pos
    target = owner_d * spots + place
    target_row = row_of(target, all_rows)
    here_row = row_of(jnp.where(owner_t == t.astype(F32), 1.0, 0.0), all_rows)
    route = jnp.where(iota((slots, all_rows), 0).astype(F32) == target_row, 1.0, 0.0)
    wide_lane = iota((all_rows, lanes), 1)
    places = jnp.where((wide_lane - 8).astype(F32) == owner_t, local + 1.0, 0.0).astype(BF16)
    beside = dot(route.astype(BF16), places)
    route = (route * here_row).astype(BF16)
    beside = beside + jnp.where(iota((slots, lanes), 1) == 1, dot(route, xg[:, feat : feat + lanes]), 0.0)
    pk[:, :feat] = dot(route, xg[:, :feat]).astype(BF16)
    pk[:, feat : feat + lanes] = beside.astype(BF16)

    def y_copy(m):
        return pltpu.make_async_remote_copy(
            src_ref=pk.at[pl.ds(pl.multiple_of(dp_at(m) * spots, spots), spots)],
            dst_ref=rx.at[pl.ds(back(m) * spots, spots)], send_sem=y_send.at[m],
            recv_sem=y_recv.at[back(m)], device_id=(dp_at(m), t, a), device_id_type=MESH)

    def y_arrival(m):
        return pltpu.make_async_remote_copy(
            src_ref=pk.at[pl.ds(pl.multiple_of(dp_at(m) * spots, spots), spots)],
            dst_ref=rx.at[pl.ds(m * spots, spots)], send_sem=y_send.at[m],
            recv_sem=y_recv.at[m], device_id=(dp_at(m), t, a), device_id_type=MESH)

    for m in range(1, nd):
        y_copy(m).start()
    rx[0:spots, :] = pk[pl.ds(pl.multiple_of(d * spots, spots), spots), :]

    def u_copy(k):
        return pltpu.make_async_remote_copy(
            src_ref=upp.at[lax.rem(t + k, nt)], dst_ref=upg.at[t], send_sem=u_send.at[k],
            recv_sem=u_recv.at[k], device_id=z_dev(k), device_id_type=MESH)

    def u_start(k, c):
        u_copy(k).start()
        return c
    lax.fori_loop(1, nt, u_start, 0)

    def f_copy(m):
        return pltpu.make_async_remote_copy(
            src_ref=ret_tx.at[m], dst_ref=ret_rx.at[back(m)], send_sem=f_send.at[m],
            recv_sem=f_recv.at[back(m)], device_id=(dp_at(m), t, a), device_id_type=MESH)

    def f_arrival(m):
        return pltpu.make_async_remote_copy(
            src_ref=ret_tx.at[m], dst_ref=ret_rx.at[m], send_sem=f_send.at[m],
            recv_sem=f_recv.at[m], device_id=(dp_at(m), t, a), device_id_type=MESH)

    def swapped(v):
        return jnp.concatenate([v[:, half:], v[:, :half]], axis=1)

    def packed(run):
        lo, hi = run
        return pl.ds(lo * spots // 2, (hi - lo) * spots // 2)

    def p_copy(c, k):
        return pltpu.make_async_remote_copy(
            src_ref=ptx.at[packed(runs[c])], dst_ref=prx.at[k, packed(runs[c])], send_sem=p_send.at[c, k],
            recv_sem=p_recv.at[c, k], device_id=x_dev(k), device_id_type=MESH)

    def r_copy(c, k, block):
        part = redg.at[block, packed(runs[c])]
        return pltpu.make_async_remote_copy(
            src_ref=part, dst_ref=part, send_sem=r_send.at[c, k],
            recv_sem=r_recv.at[c, k], device_id=z_dev(k), device_id_type=MESH)

    for c, (lo, hi) in enumerate(runs):
        n = (hi - lo) * spots
        part = slice(lo * spots, hi * spots)
        for m in range(max(lo, 1), hi):
            y_arrival(m).wait_recv()
        shrunk = dot_t(rx[part, :feat], downp[...])
        at = iota((n, lanes), 1)
        shrunk = jnp.where((at // half).astype(F32) == rx[part, feat + 1 : feat + 2].astype(F32), shrunk, 0.0)
        shrunk = shrunk + swapped(shrunk)
        shrunk = jnp.where(at[: n // 2] < half, shrunk[: n // 2], shrunk[n // 2 :])
        ptx[packed((lo, hi)), :] = shrunk.astype(BF16)
        for k in range(1, na):
            p_copy(c, k).start()
        for k in range(1, na):
            p_copy(c, k).wait_recv()
            shrunk = shrunk + prx[k, packed((lo, hi)), :].astype(F32)
        redg[t, packed((lo, hi)), :] = shrunk.astype(BF16)

        def r_start(k, s, c=c):
            r_copy(c, k, t).start()
            return s
        lax.fori_loop(1, nt, r_start, 0)

        def r_wait(k, s, c=c):
            r_copy(c, k, lax.rem(t - k + nt, nt)).wait_recv()
            if c == 0:
                u_copy(k).wait_recv()
            return s
        lax.fori_loop(1, nt, r_wait, 0)
        for g in range(nt):
            both = redg[g, packed((lo, hi)), :].astype(F32)
            turned = swapped(both)
            low = at[: n // 2] < half
            spread = jnp.concatenate([jnp.where(low, both, turned), jnp.where(low, turned, both)], axis=0)
            held = rx[part, feat + 8 + g : feat + 9 + g].astype(F32) - 1.0
            spread = jnp.where((at // half).astype(F32) == held, spread, 0.0).astype(BF16)
            grown = dot(spread, upg[g]).astype(BF16)
            ret_tx[lo:hi, g, :, :] = grown.reshape(hi - lo, spots, cols)
        for m in range(max(lo, 1), hi):
            f_copy(m).start()
    ret_rx[0] = ret_tx[0]

    fetches[8].wait()
    x = xg[:, :feat]

    def b_copy(k):
        return pltpu.make_async_remote_copy(
            src_ref=btx.at[k], dst_ref=brx.at[k], send_sem=b_send.at[k],
            recv_sem=b_recv.at[k], device_id=x_dev(k), device_id_type=MESH)
    for k in range(1, na):
        part = pl.ds(pl.multiple_of(lax.rem(a + k, na) * cols, cols), cols)
        btx[k] = dot(x, w_ref[:, part]).astype(BF16)
        b_copy(k).start()
    acc[...] = dot(x, w_ref[:, pl.ds(pl.multiple_of(a * cols, cols), cols)])
    for k in range(1, na):
        b_copy(k).wait_recv()
        acc[...] += brx[k].astype(F32)

    target = owners * spots + place
    total = acc[...]
    span = nt * spots
    for m in range(nd):
        if m:
            f_arrival(m).wait_recv()
        place_of = (iota((all_rows, span), 1) + dp_at(m) * span).astype(F32)
        pick = jnp.where(place_of == target, 1.0, 0.0).astype(BF16)
        total = total + dot(pick, ret_rx[m].reshape(span, cols))
    out_ref[...] = total.astype(BF16)

    def drain_z(k, c):
        z_copy(k, t).wait_send()
        u_copy(k).wait_send()
        for r in range(len(runs)):
            r_copy(r, k, t).wait_send()
        return c
    lax.fori_loop(1, nt, drain_z, 0)
    for m in range(1, nd):
        y_copy(m).wait_send()
        f_copy(m).wait_send()
    for k in range(1, na):
        b_copy(k).wait_send()
        for c in range(len(runs)):
            p_copy(c, k).wait_send()


def body(sizes, q, kc, vc, lengths, index, table, w, down, up):
    nd, nt, na = sizes
    rows, groups, _, width = q.shape
    cache = kc.shape[1]
    holding, rank = down.shape[0], down.shape[1]
    feat = groups * width
    columns = w.shape[-1]
    cols = columns // na
    spots = nt * CAP
    slots = nd * spots
    wide = feat + holding * rank
    hr = holding * rank
    parts = len(order_of(nd // 2)[1])
    dma = pltpu.SemaphoreType.DMA
    return pl.pallas_call(
        functools.partial(kernel, nd, nt, na, groups, cache, holding),
        out_shape=jax.ShapeDtypeStruct((nt * rows, cols), BF16),
        in_specs=[pl.BlockSpec(memory_space=pltpu.HBM)] * 9,
        out_specs=pl.BlockSpec(memory_space=pltpu.VMEM),
        scratch_shapes=[
            pltpu.VMEM((rows * groups, width), BF16),
            pltpu.VMEM((rows * cache, width), BF16),
            pltpu.VMEM((rows * cache, width), BF16),
            pltpu.VMEM((1, rows), jnp.int32),
            pltpu.VMEM((1, rows), jnp.int32),
            pltpu.VMEM((1, table.shape[0]), jnp.int32),
            pltpu.VMEM((hr * groups, width), BF16),
            pltpu.VMEM((hr * nt, cols), BF16),
            pltpu.VMEM((nt * rows, wide), BF16),
            pltpu.VMEM((slots, wide), BF16),
            pltpu.VMEM((slots, wide), BF16),
            pltpu.VMEM((feat, columns), BF16),
            pltpu.VMEM((hr, feat), BF16),
            pltpu.VMEM((nt, hr, cols), BF16),
            pltpu.VMEM((nt, hr, cols), BF16),
            pltpu.VMEM((na, nt * rows, cols), BF16),
            pltpu.VMEM((na, nt * rows, cols), BF16),
            pltpu.VMEM((nt * rows, cols), F32),
            pltpu.VMEM((slots // 2, hr), BF16),
            pltpu.VMEM((na, slots // 2, hr), BF16),
            pltpu.VMEM((nt, slots // 2, hr), BF16),
            pltpu.VMEM((nd, nt, spots, cols), BF16),
            pltpu.VMEM((nd, nt, spots, cols), BF16),
            dma((9,)),
            dma((nt,)), dma((nt,)), dma((nt,)), dma((nt,)),
            dma((nd,)), dma((nd,)),
            dma((na,)), dma((na,)), dma((parts, na)), dma((parts, na)),
            dma((parts, nt)), dma((parts, nt)),
            dma((nd,)), dma((nd,)),
        ],
        compiler_params=pltpu.CompilerParams(
            collective_id=0, has_side_effects=True, vmem_limit_bytes=60 * 1024 * 1024
        ),
    )(
        q.reshape(rows * groups, width),
        kc.reshape(rows * cache, width),
        vc.reshape(rows * cache, width),
        lengths.reshape(1, rows),
        index.reshape(1, rows),
        table.reshape(1, -1),
        w.reshape(feat, columns),
        down.reshape(hr * groups, width),
        up.reshape(hr * nt, cols),
    )


def solution(mesh):
    sizes = tuple(mesh.shape[name] for name in ("dp", "tensor", "adapter"))
    return jax.shard_map(
        functools.partial(body, sizes),
        mesh=mesh,
        in_specs=(
            P(("dp", "tensor"), None, "adapter", None),
            P(("dp", "tensor"), None, "adapter", None),
            P(("dp", "tensor"), None, "adapter", None),
            P(("dp", "tensor")),
            P(("dp", "tensor")),
            P(),
            P(None, "adapter", None, "tensor"),
            P(("dp", "tensor"), None, None, "adapter", None),
            P(("dp", "tensor"), None, None, "adapter"),
        ),
        out_specs=P("dp", ("tensor", "adapter")),
        check_vma=False,
    )
```

```python
import functools

import jax
import jax.numpy as jnp
from jax import lax
from jax.experimental import pallas as pl
from jax.experimental.pallas import tpu as pltpu
from jax.sharding import PartitionSpec as P

MESH = pl.DeviceIdType.MESH
CAP = 2
F32 = jnp.float32
BF16 = jnp.bfloat16


def iota(shape, dim):
    return lax.broadcasted_iota(jnp.int32, shape, dim)


def dot(a, b):
    return jnp.dot(a, b, preferred_element_type=F32)


def dot_t(a, b):
    return lax.dot_general(a, b, (((1,), (1,)), ((), ())), preferred_element_type=F32)


def regroup(rows, groups):
    n = rows * groups
    out, into = iota((n, n), 0), iota((n, n), 1)
    return jnp.where(into == (out % rows) * groups + out // rows, 1.0, 0.0).astype(BF16)


def column_of(row, n):
    return jnp.sum(jnp.where(iota((n, n), 0) == iota((n, n), 1), row, 0.0), axis=1, keepdims=True)


def row_of(column, n):
    return jnp.sum(jnp.where(iota((n, n), 0) == iota((n, n), 1), column, 0.0), axis=0, keepdims=True)


def attend(q_ref, k_ref, v_ref, length_row, rows, groups, cache):
    per = 128 // cache if rows * cache > 128 else rows
    width = per * cache
    lengths = jnp.sum(
        jnp.where(iota((rows * groups, rows), 0) // groups == iota((rows * groups, rows), 1), length_row, 0.0),
        axis=1,
        keepdims=True,
    )
    outs = []
    for first in range(0, rows, per):
        q = q_ref[first * groups : (first + per) * groups, :]
        k = k_ref[first * cache : (first + per) * cache, :]
        v = v_ref[first * cache : (first + per) * cache, :]
        shape = (per * groups, width)
        lane = iota(shape, 1)
        live = (iota(shape, 0) // groups == lane // cache) & (
            (lane % cache).astype(F32) < lengths[first * groups : (first + per) * groups, :]
        )
        scores = jnp.where(live, dot_t(q, k) * (q.shape[-1] ** -0.5), -1e30)
        weights = jnp.exp(scores - jnp.max(scores, axis=1, keepdims=True))
        weights = jnp.where(live, weights, 0.0)
        weights = (weights / jnp.sum(weights, axis=1, keepdims=True)).astype(BF16)
        outs.append(dot(weights, v).astype(BF16))
    return jnp.concatenate(outs, axis=0)


def order_of(chips):
    far = chips // 2
    near = [0, 1, -1, 2, -2] + list(range(3, far + 1)) + [-j for j in range(3, far)]
    return near, [(0, 6), (6, 10), (10, 2 * chips)]


def sign(j):
    return (j > 0) - (j < 0)


def kernel(
    nd, nt, na, groups, cache, holding,
    q_hbm, k_hbm, v_hbm, len_hbm, idx_hbm, slot_hbm, w_hbm, down_hbm, up_hbm, out_ref,
    q_ref, k_ref, v_ref, len_ref, idx_ref, slot_ref, down_ref, up_ref,
    xg, pk, rx, w_ref, downp, upp, upg, btx, brx, acc, ptx, prx, redg, ret_tx, ret_rx,
    in_sem, z_send, z_recv, u_send, u_recv, y_send, y_recv, b_send, b_recv, p_send, p_recv,
    r_send, r_recv, f_send, f_recv, d_send, d_recv, v_send, v_recv,
):
    d, t, a = lax.axis_index("dp"), lax.axis_index("tensor"), lax.axis_index("adapter")
    rows = q_ref.shape[0] // groups
    feat = groups * 128
    spots = nt * CAP
    slots = nd * spots
    half = 64
    lanes = 2 * half
    all_rows = nt * rows
    cols = acc.shape[1]
    chips = nd // 2
    near, runs = order_of(chips)
    chip, core = d // 2, d % 2

    def at_chip(j, m):
        return 2 * lax.rem(chip + j + chips, chips) + lax.rem(core + m % 2, 2)

    def owner_at(m):
        return at_chip(near[m // 2], m)

    def server_at(m):
        return at_chip(near[m // 2] - sign(near[m // 2]), m)

    def served_at(m):
        return at_chip(sign(near[m // 2]) - near[m // 2], m)

    def maps_of(lo, hi):
        found = []
        for m in range(lo, hi):
            side = (0, 1, 2)[sign(near[m // 2])]
            if found and found[-1][2] == side:
                found[-1][1] = m + 1
            else:
                found.append([m, m + 1, side])
        return found

    def z_dev(k):
        return (d, lax.rem(t + k, nt), a)

    def x_dev(k):
        return (d, t, lax.rem(a + k, na))

    fetches = [
        pltpu.make_async_copy(src, dst, in_sem.at[n])
        for n, (src, dst) in enumerate((
            (up_hbm, up_ref), (down_hbm, down_ref), (idx_hbm, idx_ref), (slot_hbm, slot_ref), (len_hbm, len_ref),
            (q_hbm, q_ref), (k_hbm, k_ref), (v_hbm, v_ref), (w_hbm, w_ref)))
    ]
    for fetch in fetches:
        fetch.start()
    barrier = pltpu.get_barrier_semaphore()

    def greet_z(k, c):
        pl.semaphore_signal(barrier, inc=1, device_id=z_dev(k), device_id_type=MESH)
        return c

    def greet_y(k, c):
        pl.semaphore_signal(barrier, inc=1, device_id=(lax.rem(d + k, nd), t, a), device_id_type=MESH)
        return c

    def greet_x(k, c):
        pl.semaphore_signal(barrier, inc=1, device_id=x_dev(k), device_id_type=MESH)
        return c
    lax.fori_loop(1, nt, greet_z, 0)
    lax.fori_loop(1, nd, greet_y, 0)
    lax.fori_loop(1, na, greet_x, 0)

    fetches[0].wait()
    fetches[1].wait()
    step = 256 // groups
    swap_w = regroup(step, groups)
    for b in range(holding * half // step):
        part = slice(b * step * groups, (b + 1) * step * groups)
        up = dot(swap_w, up_ref[part, :]).astype(BF16)
        for g in range(nt):
            upp[g, b * step : (b + 1) * step, :] = up[g * step : (g + 1) * step, :]
        down = dot(swap_w, down_ref[part, :]).astype(BF16)
        for g in range(groups):
            downp[0, b * step : (b + 1) * step, g * 128 : (g + 1) * 128] = down[g * step : (g + 1) * step, :]
    upg[0, t] = upp[t]

    pl.semaphore_wait(barrier, (nt - 1) + (nd - 1) + (na - 1))

    def u_copy(k):
        return pltpu.make_async_remote_copy(
            src_ref=upp.at[lax.rem(t + k, nt)], dst_ref=upg.at[0, t], send_sem=u_send.at[k],
            recv_sem=u_recv.at[k], device_id=z_dev(k), device_id_type=MESH)

    def u_arrival(k):
        return pltpu.make_async_remote_copy(
            src_ref=upp.at[lax.rem(t + k, nt)], dst_ref=upg.at[0, lax.rem(t - k + nt, nt)], send_sem=u_send.at[k],
            recv_sem=u_recv.at[k], device_id=z_dev(k), device_id_type=MESH)

    def beside_dev(side):
        return (at_chip(1 if side == 1 else -1, 0), t, a)

    def d_copy(side):
        return pltpu.make_async_remote_copy(
            src_ref=downp.at[0], dst_ref=downp.at[3 - side], send_sem=d_send.at[side],
            recv_sem=d_recv.at[3 - side], device_id=beside_dev(side), device_id_type=MESH)

    def v_copy(side, k):
        block = lax.rem(t - k + nt, nt)
        return pltpu.make_async_remote_copy(
            src_ref=upg.at[0, block], dst_ref=upg.at[3 - side, block], send_sem=v_send.at[side, k],
            recv_sem=v_recv.at[3 - side, k], device_id=beside_dev(side), device_id_type=MESH)

    for side in (1, 2):
        d_copy(side).start()
        v_copy(side, 0).start()

    for fetch in fetches[2:8]:
        fetch.wait()
    idx_col = column_of(idx_ref[...].astype(F32), rows)
    table = slot_ref.shape[1]
    slot_col = jnp.sum(
        jnp.where(idx_col == iota((rows, table), 1).astype(F32), slot_ref[...].astype(F32), 0.0),
        axis=1, keepdims=True,
    )
    owner_col = jnp.floor(slot_col * (1.0 / holding))
    local_col = slot_col - holding * owner_col
    owner_row = row_of(owner_col, rows)
    earlier = (owner_row == owner_col) & (iota((rows, rows), 1) < iota((rows, rows), 0))
    pos_col = jnp.sum(jnp.where(earlier, 1.0, 0.0), axis=1, keepdims=True)
    lane = iota((rows, lanes), 1)
    tags = jnp.where(lane == 0, owner_col * CAP + pos_col, jnp.where(lane == 1, local_col, 0.0))

    att = attend(q_ref, k_ref, v_ref, len_ref[...].astype(F32), rows, groups, cache)
    swap = regroup(rows, groups)
    att = dot(swap, att).astype(BF16)
    mine = pl.ds(pl.multiple_of(t * rows, rows), rows)
    for g in range(groups):
        xg[mine, g * 128 : (g + 1) * 128] = att[g * rows : (g + 1) * rows, :]
    xg[mine, feat : feat + lanes] = tags.astype(BF16)

    def z_copy(k, hop):
        block = lax.rem(t - k + nt, nt)
        part = xg.at[pl.ds(pl.multiple_of(block * rows, rows), rows)]
        far = (k + hop) % nt
        return pltpu.make_async_remote_copy(
            src_ref=part, dst_ref=part, send_sem=z_send.at[far], recv_sem=z_recv.at[far],
            device_id=z_dev(hop % nt), device_id_type=MESH)

    def z_arrival(k):
        block = lax.rem(t - k + nt, nt)
        part = xg.at[pl.ds(pl.multiple_of(block * rows, rows), rows)]
        return pltpu.make_async_remote_copy(
            src_ref=part, dst_ref=part, send_sem=z_send.at[k], recv_sem=z_recv.at[k],
            device_id=z_dev(k), device_id_type=MESH)

    z_first = [(0, 2), (0, -2), (0, 1), (0, -1)]
    z_second = {2: [(2, 2), (2, 1)], nt - 2: [(nt - 2, -1)]}
    for k, hop in z_first:
        z_copy(k, hop).start()
    for k, copies in z_second.items():
        z_arrival(k).wait_recv()
        for block, hop in copies:
            z_copy(block, hop).start()

    for k in range(1, nt):
        if k not in z_second:
            z_arrival(k).wait_recv()

    tag = xg[:, feat : feat + lanes].astype(F32)
    codes, local = tag[:, 0:1], tag[:, 1:2]
    owners = jnp.floor(codes * (1.0 / CAP))
    pos = codes - CAP * owners
    owner_d = jnp.floor(owners * (1.0 / nt))
    owner_t = owners - nt * owner_d
    place = (iota((all_rows, 1), 0) // rows).astype(F32) * CAP + pos
    target = owner_d * spots + place
    target_row = row_of(target, all_rows)
    here_row = row_of(jnp.where(owner_t == t.astype(F32), 1.0, 0.0), all_rows)
    route = jnp.where(iota((slots, all_rows), 0).astype(F32) == target_row, 1.0, 0.0)
    wide_lane = iota((all_rows, lanes), 1)
    places = jnp.where((wide_lane - 8).astype(F32) == owner_t, local + 1.0, 0.0).astype(BF16)
    beside = dot(route.astype(BF16), places)
    route = (route * here_row).astype(BF16)
    beside = beside + jnp.where(iota((slots, lanes), 1) == 1, dot(route, xg[:, feat : feat + lanes]), 0.0)
    pk[:, :feat] = dot(route, xg[:, :feat]).astype(BF16)
    pk[:, feat : feat + lanes] = beside.astype(BF16)

    def y_copy(m):
        return pltpu.make_async_remote_copy(
            src_ref=pk.at[pl.ds(pl.multiple_of(owner_at(m) * spots, spots), spots)],
            dst_ref=rx.at[pl.ds(m * spots, spots)], send_sem=y_send.at[m],
            recv_sem=y_recv.at[m], device_id=(server_at(m), t, a), device_id_type=MESH)

    own = [m for m in range(nd) if m % 2 == 0 and abs(near[m // 2]) < 2]
    others = [m for m in range(nd) if m not in own]
    for m in others:
        y_copy(m).start()
    near_z = sorted(range(1, nt), key=lambda k: min(k, nt - k))
    for k in near_z:
        u_copy(k).start()

    def hand_on(first, last):
        for k in near_z[first:last]:
            u_arrival(k).wait_recv()
            for side in (1, 2):
                v_copy(side, k).start()

    fetches[8].wait()
    x = xg[:, :feat]
    for k in range(1, na):
        part = pl.ds(pl.multiple_of(lax.rem(a + k, na) * cols, cols), cols)
        btx[k] = dot(x, w_ref[:, part]).astype(BF16)
    for m in own:
        rx[m * spots : (m + 1) * spots, :] = pk[pl.ds(pl.multiple_of(owner_at(m) * spots, spots), spots), :]

    def f_copy(m):
        return pltpu.make_async_remote_copy(
            src_ref=ret_tx.at[m], dst_ref=ret_rx.at[m], send_sem=f_send.at[m],
            recv_sem=f_recv.at[m], device_id=(served_at(m), t, a), device_id_type=MESH)

    def swapped(v):
        return jnp.concatenate([v[:, half:], v[:, :half]], axis=1)

    def packed(run):
        lo, hi = run
        return pl.ds(lo * spots // 2, (hi - lo) * spots // 2)

    def p_copy(c, k):
        return pltpu.make_async_remote_copy(
            src_ref=ptx.at[packed(runs[c])], dst_ref=prx.at[k, packed(runs[c])], send_sem=p_send.at[c, k],
            recv_sem=p_recv.at[c, k], device_id=x_dev(k), device_id_type=MESH)

    def r_copy(c, k, block):
        part = redg.at[block, packed(runs[c])]
        return pltpu.make_async_remote_copy(
            src_ref=part, dst_ref=part, send_sem=r_send.at[c, k],
            recv_sem=r_recv.at[c, k], device_id=z_dev(k), device_id_type=MESH)

    def down_of(c):
        lo, hi = runs[c]
        n = (hi - lo) * spots
        for m in range(lo, hi):
            if m in others:
                y_copy(m).wait_recv()
        if c == 0:
            for side in (1, 2):
                d_copy(side).wait_recv()
        shrunk = jnp.concatenate(
            [dot_t(rx[first * spots : last * spots, :feat], downp[side]) for first, last, side in maps_of(lo, hi)], axis=0)
        at = iota((n, lanes), 1)
        held = rx[lo * spots : hi * spots, feat + 1 : feat + 2].astype(F32)
        shrunk = jnp.where((at // half).astype(F32) == held, shrunk, 0.0)
        shrunk = shrunk + swapped(shrunk)
        shrunk = jnp.where(at[: n // 2] < half, shrunk[: n // 2], shrunk[n // 2 :])
        ptx[packed(runs[c]), :] = shrunk.astype(BF16)
        for k in range(1, na):
            p_copy(c, k).start()
        return shrunk

    def sum_of(c, shrunk):
        for k in range(1, na):
            p_copy(c, k).wait_recv()
            shrunk = shrunk + prx[k, packed(runs[c]), :].astype(F32)
        redg[t, packed(runs[c]), :] = shrunk.astype(BF16)

        def r_start(k, s):
            r_copy(c, k, t).start()
            return s
        lax.fori_loop(1, nt, r_start, 0)

    def up_of(c):
        lo, hi = runs[c]
        n = (hi - lo) * spots

        def r_wait(k, s):
            r_copy(c, k, lax.rem(t - k + nt, nt)).wait_recv()
            return s
        lax.fori_loop(1, nt, r_wait, 0)
        if c == 0:
            def v_wait(k, s):
                for side in (1, 2):
                    v_copy(side, k).wait_recv()
                return s
            lax.fori_loop(0, nt, v_wait, 0)
        at = iota((n, lanes), 1)
        low = at[: n // 2] < half
        for g in range(nt):
            both = redg[g, packed(runs[c]), :].astype(F32)
            turned = swapped(both)
            spread = jnp.concatenate([jnp.where(low, both, turned), jnp.where(low, turned, both)], axis=0)
            held = rx[lo * spots : hi * spots, feat + 8 + g : feat + 9 + g].astype(F32) - 1.0
            spread = jnp.where((at // half).astype(F32) == held, spread, 0.0).astype(BF16)
            for first, last, side in maps_of(lo, hi):
                grown = dot(spread[(first - lo) * spots : (last - lo) * spots], upg[side, g]).astype(BF16)
                ret_tx[first:last, g, :, :] = grown.reshape(last - first, spots, cols)
        for m in range(lo, hi):
            if m in others:
                f_copy(m).start()

    def b_copy(k):
        return pltpu.make_async_remote_copy(
            src_ref=btx.at[k], dst_ref=brx.at[k], send_sem=b_send.at[k],
            recv_sem=b_recv.at[k], device_id=x_dev(k), device_id_type=MESH)

    s0 = down_of(0)
    sum_of(0, s0)
    hand_on(0, 2)
    s1 = down_of(1)
    hand_on(2, 4)
    sum_of(1, s1)
    s2 = down_of(2)
    hand_on(4, 6)
    sum_of(2, s2)
    hand_on(6, nt)
    for k in range(1, na):
        b_copy(k).start()
    up_of(0)
    up_of(1)
    up_of(2)
    for m in own:
        ret_rx[m] = ret_tx[m]
    acc[...] = dot(x, w_ref[:, pl.ds(pl.multiple_of(a * cols, cols), cols)])
    for k in range(1, na):
        b_copy(k).wait_recv()
        acc[...] += brx[k].astype(F32)

    target = owners * spots + place
    total = acc[...]
    span = nt * spots
    for m in range(nd):
        if m in others:
            f_copy(m).wait_recv()
        place_of = (iota((all_rows, span), 1) + owner_at(m) * span).astype(F32)
        pick = jnp.where(place_of == target, 1.0, 0.0).astype(BF16)
        total = total + dot(pick, ret_rx[m].reshape(span, cols))
    out_ref[...] = total.astype(BF16)

    def drain_z(k, c):
        u_copy(k).wait_send()
        for r in range(len(runs)):
            r_copy(r, k, t).wait_send()
        return c
    lax.fori_loop(1, nt, drain_z, 0)
    for k, hop in z_first + [copy for copies in z_second.values() for copy in copies]:
        z_copy(k, hop).wait_send()

    def drain_v(k, c):
        for side in (1, 2):
            v_copy(side, k).wait_send()
        return c
    lax.fori_loop(0, nt, drain_v, 0)
    for side in (1, 2):
        d_copy(side).wait_send()
    for m in others:
        y_copy(m).wait_send()
        f_copy(m).wait_send()
    for k in range(1, na):
        b_copy(k).wait_send()
        for c in range(len(runs)):
            p_copy(c, k).wait_send()


def body(sizes, q, kc, vc, lengths, index, table, w, down, up):
    nd, nt, na = sizes
    rows, groups, _, width = q.shape
    cache = kc.shape[1]
    holding, rank = down.shape[0], down.shape[1]
    feat = groups * width
    columns = w.shape[-1]
    cols = columns // na
    spots = nt * CAP
    slots = nd * spots
    wide = feat + holding * rank
    hr = holding * rank
    parts = len(order_of(nd // 2)[1])
    dma = pltpu.SemaphoreType.DMA
    return pl.pallas_call(
        functools.partial(kernel, nd, nt, na, groups, cache, holding),
        out_shape=jax.ShapeDtypeStruct((nt * rows, cols), BF16),
        in_specs=[pl.BlockSpec(memory_space=pltpu.HBM)] * 9,
        out_specs=pl.BlockSpec(memory_space=pltpu.VMEM),
        scratch_shapes=[
            pltpu.VMEM((rows * groups, width), BF16),
            pltpu.VMEM((rows * cache, width), BF16),
            pltpu.VMEM((rows * cache, width), BF16),
            pltpu.VMEM((1, rows), jnp.int32),
            pltpu.VMEM((1, rows), jnp.int32),
            pltpu.VMEM((1, table.shape[0]), jnp.int32),
            pltpu.VMEM((hr * groups, width), BF16),
            pltpu.VMEM((hr * nt, cols), BF16),
            pltpu.VMEM((nt * rows, wide), BF16),
            pltpu.VMEM((slots, wide), BF16),
            pltpu.VMEM((slots, wide), BF16),
            pltpu.VMEM((feat, columns), BF16),
            pltpu.VMEM((3, hr, feat), BF16),
            pltpu.VMEM((nt, hr, cols), BF16),
            pltpu.VMEM((3, nt, hr, cols), BF16),
            pltpu.VMEM((na, nt * rows, cols), BF16),
            pltpu.VMEM((na, nt * rows, cols), BF16),
            pltpu.VMEM((nt * rows, cols), F32),
            pltpu.VMEM((slots // 2, hr), BF16),
            pltpu.VMEM((na, slots // 2, hr), BF16),
            pltpu.VMEM((nt, slots // 2, hr), BF16),
            pltpu.VMEM((nd, nt, spots, cols), BF16),
            pltpu.VMEM((nd, nt, spots, cols), BF16),
            dma((9,)),
            dma((nt,)), dma((nt,)), dma((nt,)), dma((nt,)),
            dma((nd,)), dma((nd,)),
            dma((na,)), dma((na,)), dma((parts, na)), dma((parts, na)),
            dma((parts, nt)), dma((parts, nt)),
            dma((nd,)), dma((nd,)),
            dma((3,)), dma((3,)), dma((3, nt)), dma((3, nt)),
        ],
        compiler_params=pltpu.CompilerParams(
            collective_id=0, has_side_effects=True, vmem_limit_bytes=60 * 1024 * 1024
        ),
    )(
        q.reshape(rows * groups, width),
        kc.reshape(rows * cache, width),
        vc.reshape(rows * cache, width),
        lengths.reshape(1, rows),
        index.reshape(1, rows),
        table.reshape(1, -1),
        w.reshape(feat, columns),
        down.reshape(hr * groups, width),
        up.reshape(hr * nt, cols),
    )


def solution(mesh):
    sizes = tuple(mesh.shape[name] for name in ("dp", "tensor", "adapter"))
    return jax.shard_map(
        functools.partial(body, sizes),
        mesh=mesh,
        in_specs=(
            P(("dp", "tensor"), None, "adapter", None),
            P(("dp", "tensor"), None, "adapter", None),
            P(("dp", "tensor"), None, "adapter", None),
            P(("dp", "tensor")),
            P(("dp", "tensor")),
            P(),
            P(None, "adapter", None, "tensor"),
            P(("dp", "tensor"), None, None, "adapter", None),
            P(("dp", "tensor"), None, None, "adapter"),
        ),
        out_specs=P("dp", ("tensor", "adapter")),
        check_vma=False,
    )
```

```python
import functools

import jax
import jax.numpy as jnp
from jax import lax
from jax.experimental import pallas as pl
from jax.experimental.pallas import tpu as pltpu
from jax.sharding import PartitionSpec as P

MESH = pl.DeviceIdType.MESH
CAP = 2
F32 = jnp.float32
BF16 = jnp.bfloat16


def iota(shape, dim):
    return lax.broadcasted_iota(jnp.int32, shape, dim)


def dot(a, b):
    return jnp.dot(a, b, preferred_element_type=F32)


def dot_t(a, b):
    return lax.dot_general(a, b, (((1,), (1,)), ((), ())), preferred_element_type=F32)


def regroup(rows, groups):
    n = rows * groups
    out, into = iota((n, n), 0), iota((n, n), 1)
    return jnp.where(into == (out % rows) * groups + out // rows, 1.0, 0.0).astype(BF16)


def column_of(row, n):
    return jnp.sum(jnp.where(iota((n, n), 0) == iota((n, n), 1), row, 0.0), axis=1, keepdims=True)


def row_of(column, n):
    return jnp.sum(jnp.where(iota((n, n), 0) == iota((n, n), 1), column, 0.0), axis=0, keepdims=True)


def attend(q_ref, k_ref, v_ref, length_row, rows, groups, cache):
    per = 128 // cache if rows * cache > 128 else rows
    width = per * cache
    lengths = jnp.sum(
        jnp.where(iota((rows * groups, rows), 0) // groups == iota((rows * groups, rows), 1), length_row, 0.0),
        axis=1,
        keepdims=True,
    )
    outs = []
    for first in range(0, rows, per):
        q = q_ref[first * groups : (first + per) * groups, :]
        k = k_ref[first * cache : (first + per) * cache, :]
        v = v_ref[first * cache : (first + per) * cache, :]
        shape = (per * groups, width)
        lane = iota(shape, 1)
        live = (iota(shape, 0) // groups == lane // cache) & (
            (lane % cache).astype(F32) < lengths[first * groups : (first + per) * groups, :]
        )
        scores = jnp.where(live, dot_t(q, k) * (q.shape[-1] ** -0.5), -1e30)
        weights = jnp.exp(scores - jnp.max(scores, axis=1, keepdims=True))
        weights = jnp.where(live, weights, 0.0)
        weights = (weights / jnp.sum(weights, axis=1, keepdims=True)).astype(BF16)
        outs.append(dot(weights, v).astype(BF16))
    return jnp.concatenate(outs, axis=0)


def order_of(chips):
    half = chips // 2
    near = [0, 1, -1, 2, -2] + list(range(3, half + 1)) + [-j for j in range(3, half)]
    return near, [(0, 6), (6, 10), (10, 2 * chips)]


def ring_order(n):
    return sorted(range(n), key=lambda k: min(k, n - k))


def sign(j):
    return (j > 0) - (j < 0)


def kernel(
    nd, nt, na, groups, cache, holding,
    q_hbm, k_hbm, v_hbm, len_hbm, idx_hbm, slot_hbm, w_hbm, down_hbm, up_hbm, out_ref,
    q_ref, k_ref, v_ref, len_ref, idx_ref, slot_ref, down_ref, up_ref,
    xg, tg, pk, rx, w_ref, downp, upp, upg, btx, brx, acc, ptx, prx, redg, ret_tx, ret_rx,
    in_sem, z_send, z_recv, u_send, u_recv, y_send, y_recv, b_send, b_recv, p_send, p_recv,
    r_send, r_recv, f_send, f_recv, d_send, d_recv, v_send, v_recv, t_send, t_recv,
):
    d, t, a = lax.axis_index("dp"), lax.axis_index("tensor"), lax.axis_index("adapter")
    rows = q_ref.shape[0] // groups
    feat = groups * 128
    spots = nt * CAP
    slots = nd * spots
    half = 64
    lanes = 2 * half
    all_rows = nt * rows
    cols = acc.shape[1]
    chips = nd // 2
    near, runs = order_of(chips)
    chip, core = d // 2, d % 2

    def away(m):
        j = near[m // 2]
        return -j if 2 * j == chips and m % 2 else j

    def at_chip(j, m):
        return 2 * lax.rem(chip + j + chips, chips) + lax.rem(core + m % 2, 2)

    def owner_at(m):
        return at_chip(away(m), m)

    def server_at(m):
        return at_chip(away(m) - sign(away(m)), m)

    def served_at(m):
        return at_chip(sign(away(m)) - away(m), m)

    def maps_of(lo, hi):
        found = []
        for m in range(lo, hi):
            side = (0, 1, 2)[sign(away(m))]
            if found and found[-1][2] == side:
                found[-1][1] = m + 1
            else:
                found.append([m, m + 1, side])
        return found

    def z_dev(k):
        return (d, lax.rem(t + k, nt), a)

    def x_dev(k):
        return (d, t, lax.rem(a + k, na))

    fetches = [
        pltpu.make_async_copy(src, dst, in_sem.at[n])
        for n, (src, dst) in enumerate((
            (q_hbm, q_ref), (k_hbm, k_ref), (len_hbm, len_ref), (v_hbm, v_ref), (idx_hbm, idx_ref),
            (slot_hbm, slot_ref), (up_hbm, up_ref), (down_hbm, down_ref), (w_hbm, w_ref)))
    ]
    for fetch in fetches:
        fetch.start()
    barrier = pltpu.get_barrier_semaphore()

    def greet_z(k, c):
        pl.semaphore_signal(barrier, inc=1, device_id=z_dev(k), device_id_type=MESH)
        return c

    def greet_y(k, c):
        pl.semaphore_signal(barrier, inc=1, device_id=(lax.rem(d + k, nd), t, a), device_id_type=MESH)
        return c

    def greet_x(k, c):
        pl.semaphore_signal(barrier, inc=1, device_id=x_dev(k), device_id_type=MESH)
        return c
    lax.fori_loop(1, nt, greet_z, 0)
    lax.fori_loop(1, nd, greet_y, 0)
    lax.fori_loop(1, na, greet_x, 0)

    for fetch in fetches[:4]:
        fetch.wait()
    att = attend(q_ref, k_ref, v_ref, len_ref[...].astype(F32), rows, groups, cache)
    swap = regroup(rows, groups)
    att = dot(swap, att).astype(BF16)
    for g in range(groups):
        xg[0:rows, g * 128 : (g + 1) * 128] = att[g * rows : (g + 1) * rows, :]

    pl.semaphore_wait(barrier, (nt - 1) + (nd - 1) + (na - 1))
    order_z = ring_order(nt)
    pos_z = [order_z.index(k) for k in range(nt)]

    def z_part(place):
        return xg.at[pl.ds(place * rows, rows)]

    def z_copy(place, hop, far):
        return pltpu.make_async_remote_copy(
            src_ref=z_part(place), dst_ref=z_part(pos_z[far]), send_sem=z_send.at[far], recv_sem=z_recv.at[far],
            device_id=(d, lax.rem(t + hop + nt, nt), a), device_id_type=MESH)

    def z_arrival(k):
        return pltpu.make_async_remote_copy(
            src_ref=z_part(0), dst_ref=z_part(pos_z[k]), send_sem=z_send.at[k], recv_sem=z_recv.at[k],
            device_id=z_dev(k), device_id_type=MESH)

    halfway = nt // 2
    z_first = [(0, 2, 2), (0, -2, nt - 2), (0, 1, 1), (0, -1, nt - 1)]
    z_second = [
        (pos_z[2], 1, 3), (pos_z[nt - 2], -1, nt - 3),
        (pos_z[2] + (pos_z[nt - 2] - pos_z[2]) * core, 2 - 4 * core, halfway)]
    for copy in z_first:
        z_copy(*copy).start()

    for fetch in fetches[4:6]:
        fetch.wait()
    idx_col = column_of(idx_ref[...].astype(F32), rows)
    table = slot_ref.shape[1]
    slot_col = jnp.sum(
        jnp.where(idx_col == iota((rows, table), 1).astype(F32), slot_ref[...].astype(F32), 0.0),
        axis=1, keepdims=True,
    )
    owner_col = jnp.floor(slot_col * (1.0 / holding))
    local_col = slot_col - holding * owner_col
    owner_row = row_of(owner_col, rows)
    earlier = (owner_row == owner_col) & (iota((rows, rows), 1) < iota((rows, rows), 0))
    pos_col = jnp.sum(jnp.where(earlier, 1.0, 0.0), axis=1, keepdims=True)
    lane = iota((rows, lanes), 1)
    tags = jnp.where(lane == 0, owner_col * CAP + pos_col, jnp.where(lane == 1, local_col, 0.0))

    tg[0:rows, :] = tags.astype(BF16)

    def t_copy(k):
        return pltpu.make_async_remote_copy(
            src_ref=tg.at[pl.ds(0, rows)], dst_ref=tg.at[pl.ds(pos_z[k] * rows, rows)], send_sem=t_send.at[k],
            recv_sem=t_recv.at[k], device_id=z_dev(k), device_id_type=MESH)
    for k in order_z[1:]:
        t_copy(k).start()

    fetches[6].wait()
    step = 256 // groups
    swap_w = regroup(step, groups)
    for b in range(holding * half // step):
        part = slice(b * step * groups, (b + 1) * step * groups)
        up = dot(swap_w, up_ref[part, :]).astype(BF16)
        for g in range(nt):
            upp[g, b * step : (b + 1) * step, :] = up[g * step : (g + 1) * step, :]
    upg[0, t] = upp[t]

    def u_copy(k):
        return pltpu.make_async_remote_copy(
            src_ref=upp.at[lax.rem(t + k, nt)], dst_ref=upg.at[0, t], send_sem=u_send.at[k],
            recv_sem=u_recv.at[k], device_id=z_dev(k), device_id_type=MESH)

    def u_arrival(k):
        return pltpu.make_async_remote_copy(
            src_ref=upp.at[lax.rem(t + k, nt)], dst_ref=upg.at[0, lax.rem(t - k + nt, nt)], send_sem=u_send.at[k],
            recv_sem=u_recv.at[k], device_id=z_dev(k), device_id_type=MESH)

    def beside_dev(side):
        return (at_chip(1 if side == 1 else -1, 0), t, a)

    def d_copy(side):
        return pltpu.make_async_remote_copy(
            src_ref=downp.at[0], dst_ref=downp.at[3 - side], send_sem=d_send.at[side],
            recv_sem=d_recv.at[3 - side], device_id=beside_dev(side), device_id_type=MESH)

    def v_copy(side, k):
        block = lax.rem(t - k + nt, nt)
        return pltpu.make_async_remote_copy(
            src_ref=upg.at[0, block], dst_ref=upg.at[3 - side, block], send_sem=v_send.at[side, k],
            recv_sem=v_recv.at[3 - side, k], device_id=beside_dev(side), device_id_type=MESH)

    for side in (1, 2):
        v_copy(side, 0).start()
    near_z = ring_order(nt)[1:]
    early = 2
    for k in near_z[:early]:
        u_copy(k).start()

    def hand_on(first, last):
        for k in near_z[first:last]:
            u_arrival(k).wait_recv()
            for side in (1, 2):
                v_copy(side, k).start()

    fetches[7].wait()
    for b in range(holding * half // step):
        part = slice(b * step * groups, (b + 1) * step * groups)
        down = dot(swap_w, down_ref[part, :]).astype(BF16)
        for g in range(groups):
            downp[0, b * step : (b + 1) * step, g * 128 : (g + 1) * 128] = down[g * step : (g + 1) * step, :]
    for side in (1, 2):
        d_copy(side).start()

    z_arrival(2).wait_recv()
    z_copy(*z_second[0]).start()
    z_arrival(nt - 2).wait_recv()
    z_copy(*z_second[1]).start()
    z_copy(*z_second[2]).start()
    hand_on(0, early)
    for k in order_z[1:]:
        t_copy(k).wait_recv()
    tag = tg[...].astype(F32)
    codes, local = tag[:, 0:1], tag[:, 1:2]
    owners = jnp.floor(codes * (1.0 / CAP))
    pos = codes - CAP * owners
    owner_d = jnp.floor(owners * (1.0 / nt))
    owner_t = owners - nt * owner_d
    block = iota((all_rows, 1), 0) // rows
    block = jnp.where(block % 2 == 1, (block + 1) // 2, nt - block // 2)
    place = ((t - block + nt) % nt).astype(F32) * CAP + pos
    target = owner_d * spots + place
    target_row = row_of(target, all_rows)
    here_row = row_of(jnp.where(owner_t == t.astype(F32), 1.0, 0.0), all_rows)
    route = jnp.where(iota((slots, all_rows), 0).astype(F32) == target_row, 1.0, 0.0)
    wide_lane = iota((all_rows, lanes), 1)
    places = jnp.where((wide_lane - 8).astype(F32) == owner_t, local + 1.0, 0.0).astype(BF16)
    beside = dot(route.astype(BF16), places)
    route = (route * here_row).astype(BF16)
    beside = beside + jnp.where(iota((slots, lanes), 1) == 1, dot(route, tg[...]), 0.0)
    pk[:, feat : feat + lanes] = beside.astype(BF16)

    z_arrival(1).wait_recv()
    z_arrival(nt - 1).wait_recv()

    fetches[8].wait()
    near_rows = 5 * rows

    def b_copy(k, h):
        part = pl.ds(h * near_rows, near_rows if h == 0 else all_rows - near_rows)
        return pltpu.make_async_remote_copy(
            src_ref=btx.at[k, part], dst_ref=brx.at[k, part], send_sem=b_send.at[h, k],
            recv_sem=b_recv.at[h, k], device_id=x_dev(k), device_id_type=MESH)

    def project(h):
        part = slice(0, near_rows) if h == 0 else slice(near_rows, all_rows)
        x = xg[part, :]
        for k in range(1, na):
            at = pl.ds(pl.multiple_of(lax.rem(a + k, na) * cols, cols), cols)
            btx[k, part, :] = dot(x, w_ref[:, at]).astype(BF16)
            b_copy(k, h).start()
        acc[part, :] = dot(x, w_ref[:, pl.ds(pl.multiple_of(a * cols, cols), cols)])
    project(0)
    for k in (3, nt - 3, halfway):
        z_arrival(k).wait_recv()
    pk[:, :feat] = dot(route, xg[...]).astype(BF16)

    def y_copy(m):
        return pltpu.make_async_remote_copy(
            src_ref=pk.at[pl.ds(pl.multiple_of(owner_at(m) * spots, spots), spots)],
            dst_ref=rx.at[pl.ds(m * spots, spots)], send_sem=y_send.at[m],
            recv_sem=y_recv.at[m], device_id=(server_at(m), t, a), device_id_type=MESH)

    own = [m for m in range(nd) if m % 2 == 0 and abs(away(m)) < 2]
    others = [m for m in range(nd) if m not in own]
    for m in others:
        y_copy(m).start()
    for k in near_z[early:]:
        u_copy(k).start()

    for m in own:
        rx[m * spots : (m + 1) * spots, :] = pk[pl.ds(pl.multiple_of(owner_at(m) * spots, spots), spots), :]

    def f_copy(m):
        return pltpu.make_async_remote_copy(
            src_ref=ret_tx.at[m], dst_ref=ret_rx.at[m], send_sem=f_send.at[m],
            recv_sem=f_recv.at[m], device_id=(served_at(m), t, a), device_id_type=MESH)

    def swapped(v):
        return jnp.concatenate([v[:, half:], v[:, :half]], axis=1)

    def packed(run):
        lo, hi = run
        return pl.ds(lo * spots // 2, (hi - lo) * spots // 2)

    def p_copy(c, k):
        return pltpu.make_async_remote_copy(
            src_ref=ptx.at[packed(runs[c])], dst_ref=prx.at[k, packed(runs[c])], send_sem=p_send.at[c, k],
            recv_sem=p_recv.at[c, k], device_id=x_dev(k), device_id_type=MESH)

    def r_copy(c, k, block):
        part = redg.at[block, packed(runs[c])]
        return pltpu.make_async_remote_copy(
            src_ref=part, dst_ref=part, send_sem=r_send.at[c, k],
            recv_sem=r_recv.at[c, k], device_id=z_dev(k), device_id_type=MESH)

    def down_of(c):
        lo, hi = runs[c]
        n = (hi - lo) * spots
        for m in range(lo, hi):
            if m in others:
                y_copy(m).wait_recv()
        shrunk = jnp.concatenate(
            [dot_t(rx[first * spots : last * spots, :feat], downp[side]) for first, last, side in maps_of(lo, hi)], axis=0)
        at = iota((n, lanes), 1)
        held = rx[lo * spots : hi * spots, feat + 1 : feat + 2].astype(F32)
        shrunk = jnp.where((at // half).astype(F32) == held, shrunk, 0.0)
        shrunk = shrunk + swapped(shrunk)
        shrunk = jnp.where(at[: n // 2] < half, shrunk[: n // 2], shrunk[n // 2 :])
        ptx[packed(runs[c]), :] = shrunk.astype(BF16)
        for k in range(1, na):
            p_copy(c, k).start()
        return shrunk

    def sum_of(c, shrunk):
        for k in range(1, na):
            p_copy(c, k).wait_recv()
            shrunk = shrunk + prx[k, packed(runs[c]), :].astype(F32)
        redg[t, packed(runs[c]), :] = shrunk.astype(BF16)

        def r_start(k, s):
            r_copy(c, k, t).start()
            return s
        lax.fori_loop(1, nt, r_start, 0)

    def up_of(c):
        lo, hi = runs[c]
        n = (hi - lo) * spots

        def r_wait(k, s):
            r_copy(c, k, lax.rem(t - k + nt, nt)).wait_recv()
            return s
        lax.fori_loop(1, nt, r_wait, 0)
        if c == 0:
            def v_wait(k, s):
                for side in (1, 2):
                    v_copy(side, k).wait_recv()
                return s
            lax.fori_loop(0, nt, v_wait, 0)
        at = iota((n, lanes), 1)
        low = at[: n // 2] < half
        for g in range(nt):
            both = redg[g, packed(runs[c]), :].astype(F32)
            turned = swapped(both)
            spread = jnp.concatenate([jnp.where(low, both, turned), jnp.where(low, turned, both)], axis=0)
            held = rx[lo * spots : hi * spots, feat + 8 + g : feat + 9 + g].astype(F32) - 1.0
            spread = jnp.where((at // half).astype(F32) == held, spread, 0.0).astype(BF16)
            for first, last, side in maps_of(lo, hi):
                grown = dot(spread[(first - lo) * spots : (last - lo) * spots], upg[side, g]).astype(BF16)
                ret_tx[first:last, g, :, :] = grown.reshape(last - first, spots, cols)
        for m in range(lo, hi):
            if m in others:
                f_copy(m).start()

    for side in (1, 2):
        d_copy(side).wait_recv()
    near_sum = down_of(0)
    sum_of(0, near_sum)
    hand_on(early, 4)
    first_sum = down_of(1)
    hand_on(4, 5)
    sum_of(1, first_sum)
    hand_on(5, 6)
    next_sum = down_of(2)
    hand_on(6, nt)
    sum_of(2, next_sum)
    project(1)
    up_of(0)
    up_of(1)
    up_of(2)
    for m in own:
        ret_rx[m] = ret_tx[m]
    for h in (0, 1):
        for k in range(1, na):
            b_copy(k, h).wait_recv()
    for k in range(1, na):
        acc[...] += brx[k].astype(F32)

    target = owners * spots + place
    total = acc[...]
    span = nt * spots
    for m in range(nd):
        if m in others:
            f_copy(m).wait_recv()
        place_of = (iota((all_rows, span), 1) + owner_at(m) * span).astype(F32)
        pick = jnp.where(place_of == target, 1.0, 0.0).astype(BF16)
        total = total + dot(pick, ret_rx[m].reshape(span, cols))
    for k in range(nt):
        out_ref[pl.ds(pl.multiple_of(lax.rem(t - k + nt, nt) * rows, rows), rows), :] = total[
            pos_z[k] * rows : (pos_z[k] + 1) * rows].astype(BF16)

    def drain_z(k, c):
        u_copy(k).wait_send()
        for r in range(len(runs)):
            r_copy(r, k, t).wait_send()
        return c
    lax.fori_loop(1, nt, drain_z, 0)
    for copy in z_first + z_second:
        z_copy(*copy).wait_send()

    def drain_v(k, c):
        for side in (1, 2):
            v_copy(side, k).wait_send()
        return c
    lax.fori_loop(0, nt, drain_v, 0)
    for side in (1, 2):
        d_copy(side).wait_send()
    for k in order_z[1:]:
        t_copy(k).wait_send()
    for m in others:
        y_copy(m).wait_send()
        f_copy(m).wait_send()
    for k in range(1, na):
        b_copy(k, 0).wait_send()
        b_copy(k, 1).wait_send()
        for c in range(len(runs)):
            p_copy(c, k).wait_send()


def body(sizes, q, kc, vc, lengths, index, table, w, down, up):
    nd, nt, na = sizes
    rows, groups, _, width = q.shape
    cache = kc.shape[1]
    holding, rank = down.shape[0], down.shape[1]
    feat = groups * width
    columns = w.shape[-1]
    cols = columns // na
    spots = nt * CAP
    slots = nd * spots
    wide = feat + holding * rank
    hr = holding * rank
    parts = len(order_of(nd // 2)[1])
    dma = pltpu.SemaphoreType.DMA
    return pl.pallas_call(
        functools.partial(kernel, nd, nt, na, groups, cache, holding),
        out_shape=jax.ShapeDtypeStruct((nt * rows, cols), BF16),
        in_specs=[pl.BlockSpec(memory_space=pltpu.HBM)] * 9,
        out_specs=pl.BlockSpec(memory_space=pltpu.VMEM),
        scratch_shapes=[
            pltpu.VMEM((rows * groups, width), BF16),
            pltpu.VMEM((rows * cache, width), BF16),
            pltpu.VMEM((rows * cache, width), BF16),
            pltpu.VMEM((1, rows), jnp.int32),
            pltpu.VMEM((1, rows), jnp.int32),
            pltpu.VMEM((1, table.shape[0]), jnp.int32),
            pltpu.VMEM((hr * groups, width), BF16),
            pltpu.VMEM((hr * nt, cols), BF16),
            pltpu.VMEM((nt * rows, feat), BF16),
            pltpu.VMEM((nt * rows, hr), BF16),
            pltpu.VMEM((slots, wide), BF16),
            pltpu.VMEM((slots, wide), BF16),
            pltpu.VMEM((feat, columns), BF16),
            pltpu.VMEM((3, hr, feat), BF16),
            pltpu.VMEM((nt, hr, cols), BF16),
            pltpu.VMEM((3, nt, hr, cols), BF16),
            pltpu.VMEM((na, nt * rows, cols), BF16),
            pltpu.VMEM((na, nt * rows, cols), BF16),
            pltpu.VMEM((nt * rows, cols), F32),
            pltpu.VMEM((slots // 2, hr), BF16),
            pltpu.VMEM((na, slots // 2, hr), BF16),
            pltpu.VMEM((nt, slots // 2, hr), BF16),
            pltpu.VMEM((nd, nt, spots, cols), BF16),
            pltpu.VMEM((nd, nt, spots, cols), BF16),
            dma((9,)),
            dma((nt,)), dma((nt,)), dma((nt,)), dma((nt,)),
            dma((nd,)), dma((nd,)),
            dma((2, na)), dma((2, na)), dma((parts, na)), dma((parts, na)),
            dma((parts, nt)), dma((parts, nt)),
            dma((nd,)), dma((nd,)),
            dma((3,)), dma((3,)), dma((3, nt)), dma((3, nt)),
            dma((nt,)), dma((nt,)),
        ],
        compiler_params=pltpu.CompilerParams(
            collective_id=0, has_side_effects=True, vmem_limit_bytes=60 * 1024 * 1024
        ),
    )(
        q.reshape(rows * groups, width),
        kc.reshape(rows * cache, width),
        vc.reshape(rows * cache, width),
        lengths.reshape(1, rows),
        index.reshape(1, rows),
        table.reshape(1, -1),
        w.reshape(feat, columns),
        down.reshape(hr * groups, width),
        up.reshape(hr * nt, cols),
    )


def solution(mesh):
    sizes = tuple(mesh.shape[name] for name in ("dp", "tensor", "adapter"))
    return jax.shard_map(
        functools.partial(body, sizes),
        mesh=mesh,
        in_specs=(
            P(("dp", "tensor"), None, "adapter", None),
            P(("dp", "tensor"), None, "adapter", None),
            P(("dp", "tensor"), None, "adapter", None),
            P(("dp", "tensor")),
            P(("dp", "tensor")),
            P(),
            P(None, "adapter", None, "tensor"),
            P(("dp", "tensor"), None, None, "adapter", None),
            P(("dp", "tensor"), None, None, "adapter"),
        ),
        out_specs=P("dp", ("tensor", "adapter")),
        check_vma=False,
    )
```

```python
import functools

import jax
import jax.numpy as jnp
from jax import lax
from jax.experimental import pallas as pl
from jax.experimental.pallas import tpu as pltpu
from jax.sharding import PartitionSpec as P

MESH = pl.DeviceIdType.MESH
CAP = 2
F32 = jnp.float32
BF16 = jnp.bfloat16


def iota(shape, dim):
    return lax.broadcasted_iota(jnp.int32, shape, dim)


def dot(a, b):
    return jnp.dot(a, b, preferred_element_type=F32)


def dot_t(a, b):
    return lax.dot_general(a, b, (((1,), (1,)), ((), ())), preferred_element_type=F32)


def regroup(rows, groups):
    n = rows * groups
    out, into = iota((n, n), 0), iota((n, n), 1)
    return jnp.where(into == (out % rows) * groups + out // rows, 1.0, 0.0).astype(BF16)


def column_of(row, n):
    return jnp.sum(jnp.where(iota((n, n), 0) == iota((n, n), 1), row, 0.0), axis=1, keepdims=True)


def row_of(column, n):
    return jnp.sum(jnp.where(iota((n, n), 0) == iota((n, n), 1), column, 0.0), axis=0, keepdims=True)


def attend(q_ref, k_ref, v_ref, length_row, rows, groups, cache):
    per = 128 // cache if rows * cache > 128 else rows
    width = per * cache
    lengths = jnp.sum(
        jnp.where(iota((rows * groups, rows), 0) // groups == iota((rows * groups, rows), 1), length_row, 0.0),
        axis=1,
        keepdims=True,
    )
    outs = []
    for first in range(0, rows, per):
        q = q_ref[first * groups : (first + per) * groups, :]
        k = k_ref[first * cache : (first + per) * cache, :]
        v = v_ref[first * cache : (first + per) * cache, :]
        shape = (per * groups, width)
        lane = iota(shape, 1)
        live = (iota(shape, 0) // groups == lane // cache) & (
            (lane % cache).astype(F32) < lengths[first * groups : (first + per) * groups, :]
        )
        scores = jnp.where(live, dot_t(q, k) * (q.shape[-1] ** -0.5), -1e30)
        weights = jnp.exp(scores - jnp.max(scores, axis=1, keepdims=True))
        weights = jnp.where(live, weights, 0.0)
        weights = (weights / jnp.sum(weights, axis=1, keepdims=True)).astype(BF16)
        outs.append(dot(weights, v).astype(BF16))
    return jnp.concatenate(outs, axis=0)


def order_of(chips):
    half = chips // 2
    near = [0, 1, -1, 2, -2] + list(range(3, half + 1)) + [-j for j in range(3, half)]
    return near, [(0, 6), (6, 10), (10, 2 * chips)]


def ring_order(n):
    return sorted(range(n), key=lambda k: min(k, n - k))


def sign(j):
    return (j > 0) - (j < 0)


def kernel(
    nd, nt, na, groups, cache, holding,
    q_hbm, k_hbm, v_hbm, len_hbm, idx_hbm, slot_hbm, w_hbm, down_hbm, up_hbm, out_ref,
    q_ref, k_ref, v_ref, len_ref, idx_ref, slot_ref, down_ref, up_ref,
    xg, tg, pk, rx, w_ref, downp, upp, upg, btx, brx, acc, ptx, prx, redg, ret_tx, ret_rx,
    in_sem, z_send, z_recv, u_send, u_recv, y_send, y_recv, b_send, b_recv, p_send, p_recv,
    r_send, r_recv, f_send, f_recv, d_send, d_recv, v_send, v_recv, t_send, t_recv,
):
    d, t, a = lax.axis_index("dp"), lax.axis_index("tensor"), lax.axis_index("adapter")
    rows = q_ref.shape[0] // groups
    feat = groups * 128
    spots = nt * CAP
    slots = nd * spots
    half = 64
    lanes = 2 * half
    all_rows = nt * rows
    cols = acc.shape[1]
    chips = nd // 2
    near, runs = order_of(chips)
    chip, core = d // 2, d % 2

    def away(m):
        j = near[m // 2]
        return -j if 2 * j == chips and m % 2 else j

    def at_chip(j, m):
        return 2 * lax.rem(chip + j + chips, chips) + lax.rem(core + m % 2, 2)

    def owner_at(m):
        return at_chip(away(m), m)

    def server_at(m):
        return at_chip(away(m) - sign(away(m)), m)

    def served_at(m):
        return at_chip(sign(away(m)) - away(m), m)

    def maps_of(lo, hi):
        found = []
        for m in range(lo, hi):
            side = (0, 1, 2)[sign(away(m))]
            if found and found[-1][2] == side:
                found[-1][1] = m + 1
            else:
                found.append([m, m + 1, side])
        return found

    def z_dev(k):
        return (d, lax.rem(t + k, nt), a)

    def x_dev(k):
        return (d, t, lax.rem(a + k, na))

    fetches = [
        pltpu.make_async_copy(src, dst, in_sem.at[n])
        for n, (src, dst) in enumerate((
            (q_hbm, q_ref), (k_hbm, k_ref), (len_hbm, len_ref), (v_hbm, v_ref), (idx_hbm, idx_ref),
            (slot_hbm, slot_ref), (up_hbm, up_ref), (down_hbm, down_ref), (w_hbm, w_ref)))
    ]
    for fetch in fetches:
        fetch.start()
    barrier = pltpu.get_barrier_semaphore()

    def greet_z(k, c):
        pl.semaphore_signal(barrier, inc=1, device_id=z_dev(k), device_id_type=MESH)
        return c

    def greet_y(k, c):
        pl.semaphore_signal(barrier, inc=1, device_id=(lax.rem(d + k, nd), t, a), device_id_type=MESH)
        return c

    def greet_x(k, c):
        pl.semaphore_signal(barrier, inc=1, device_id=x_dev(k), device_id_type=MESH)
        return c
    lax.fori_loop(1, nt, greet_z, 0)
    lax.fori_loop(1, nd, greet_y, 0)
    lax.fori_loop(1, na, greet_x, 0)

    for fetch in fetches[:4]:
        fetch.wait()
    att = attend(q_ref, k_ref, v_ref, len_ref[...].astype(F32), rows, groups, cache)
    swap = regroup(rows, groups)
    att = dot(swap, att).astype(BF16)
    for g in range(groups):
        xg[0:rows, g * 128 : (g + 1) * 128] = att[g * rows : (g + 1) * rows, :]

    pl.semaphore_wait(barrier, (nt - 1) + (nd - 1) + (na - 1))
    order_z = ring_order(nt)
    pos_z = [order_z.index(k) for k in range(nt)]

    def z_part(place):
        return xg.at[pl.ds(place * rows, rows)]

    def z_copy(place, hop, far):
        return pltpu.make_async_remote_copy(
            src_ref=z_part(place), dst_ref=z_part(pos_z[far]), send_sem=z_send.at[far], recv_sem=z_recv.at[far],
            device_id=(d, lax.rem(t + hop + nt, nt), a), device_id_type=MESH)

    def z_arrival(k):
        return pltpu.make_async_remote_copy(
            src_ref=z_part(0), dst_ref=z_part(pos_z[k]), send_sem=z_send.at[k], recv_sem=z_recv.at[k],
            device_id=z_dev(k), device_id_type=MESH)

    halfway = nt // 2
    z_first = [(0, 2, 2), (0, -2, nt - 2), (0, 1, 1), (0, -1, nt - 1)]
    z_second = [
        (pos_z[2], 1, 3), (pos_z[nt - 2], -1, nt - 3),
        (pos_z[2] + (pos_z[nt - 2] - pos_z[2]) * core, 2 - 4 * core, halfway)]
    for copy in z_first:
        z_copy(*copy).start()

    for fetch in fetches[4:6]:
        fetch.wait()
    idx_col = column_of(idx_ref[...].astype(F32), rows)
    table = slot_ref.shape[1]
    slot_col = jnp.sum(
        jnp.where(idx_col == iota((rows, table), 1).astype(F32), slot_ref[...].astype(F32), 0.0),
        axis=1, keepdims=True,
    )
    owner_col = jnp.floor(slot_col * (1.0 / holding))
    local_col = slot_col - holding * owner_col
    owner_row = row_of(owner_col, rows)
    earlier = (owner_row == owner_col) & (iota((rows, rows), 1) < iota((rows, rows), 0))
    pos_col = jnp.sum(jnp.where(earlier, 1.0, 0.0), axis=1, keepdims=True)
    lane = iota((rows, lanes), 1)
    tags = jnp.where(lane == 0, owner_col * CAP + pos_col, jnp.where(lane == 1, local_col, 0.0))

    tg[0:rows, :] = tags.astype(BF16)

    def t_copy(k):
        return pltpu.make_async_remote_copy(
            src_ref=tg.at[pl.ds(0, rows)], dst_ref=tg.at[pl.ds(pos_z[k] * rows, rows)], send_sem=t_send.at[k],
            recv_sem=t_recv.at[k], device_id=z_dev(k), device_id_type=MESH)
    for k in reversed(order_z[1:]):
        t_copy(k).start()

    fetches[6].wait()
    step = 256 // groups
    swap_w = regroup(step, groups)
    for b in range(holding * half // step):
        part = slice(b * step * groups, (b + 1) * step * groups)
        up = dot(swap_w, up_ref[part, :]).astype(BF16)
        for g in range(nt):
            upp[g, b * step : (b + 1) * step, :] = up[g * step : (g + 1) * step, :]
    upg[0, t] = upp[t]

    def u_copy(k):
        return pltpu.make_async_remote_copy(
            src_ref=upp.at[lax.rem(t + k, nt)], dst_ref=upg.at[0, t], send_sem=u_send.at[k],
            recv_sem=u_recv.at[k], device_id=z_dev(k), device_id_type=MESH)

    def u_arrival(k):
        return pltpu.make_async_remote_copy(
            src_ref=upp.at[lax.rem(t + k, nt)], dst_ref=upg.at[0, lax.rem(t - k + nt, nt)], send_sem=u_send.at[k],
            recv_sem=u_recv.at[k], device_id=z_dev(k), device_id_type=MESH)

    def beside_dev(side):
        return (at_chip(1 if side == 1 else -1, 0), t, a)

    def d_copy(side):
        return pltpu.make_async_remote_copy(
            src_ref=downp.at[0], dst_ref=downp.at[3 - side], send_sem=d_send.at[side],
            recv_sem=d_recv.at[3 - side], device_id=beside_dev(side), device_id_type=MESH)

    def v_copy(side, k):
        block = lax.rem(t - k + nt, nt)
        return pltpu.make_async_remote_copy(
            src_ref=upg.at[0, block], dst_ref=upg.at[3 - side, block], send_sem=v_send.at[side, k],
            recv_sem=v_recv.at[3 - side, k], device_id=beside_dev(side), device_id_type=MESH)

    for side in (1, 2):
        v_copy(side, 0).start()
    near_z = ring_order(nt)[1:]
    early = 2
    for k in near_z[:early]:
        u_copy(k).start()

    def hand_on(first, last):
        for k in near_z[first:last]:
            u_arrival(k).wait_recv()
            for side in (1, 2):
                v_copy(side, k).start()

    fetches[7].wait()
    for b in range(holding * half // step):
        part = slice(b * step * groups, (b + 1) * step * groups)
        down = dot(swap_w, down_ref[part, :]).astype(BF16)
        for g in range(groups):
            downp[0, b * step : (b + 1) * step, g * 128 : (g + 1) * 128] = down[g * step : (g + 1) * step, :]
    for side in (1, 2):
        d_copy(side).start()

    z_arrival(2).wait_recv()
    z_copy(*z_second[0]).start()
    z_arrival(nt - 2).wait_recv()
    z_copy(*z_second[1]).start()
    z_copy(*z_second[2]).start()
    hand_on(0, early)
    for k in order_z[1:]:
        t_copy(k).wait_recv()
    tag = tg[...].astype(F32)
    codes, local = tag[:, 0:1], tag[:, 1:2]
    owners = jnp.floor(codes * (1.0 / CAP))
    pos = codes - CAP * owners
    owner_d = jnp.floor(owners * (1.0 / nt))
    owner_t = owners - nt * owner_d
    block = iota((all_rows, 1), 0) // rows
    block = jnp.where(block % 2 == 1, (block + 1) // 2, nt - block // 2)
    place = ((t - block + nt) % nt).astype(F32) * CAP + pos
    target = owner_d * spots + place
    target_row = row_of(target, all_rows)
    here_row = row_of(jnp.where(owner_t == t.astype(F32), 1.0, 0.0), all_rows)
    route = jnp.where(iota((slots, all_rows), 0).astype(F32) == target_row, 1.0, 0.0)
    wide_lane = iota((all_rows, lanes), 1)
    places = jnp.where((wide_lane - 8).astype(F32) == owner_t, local + 1.0, 0.0).astype(BF16)
    beside = dot(route.astype(BF16), places)
    route = (route * here_row).astype(BF16)
    beside = beside + jnp.where(iota((slots, lanes), 1) == 1, dot(route, tg[...]), 0.0)
    pk[:, feat : feat + lanes] = beside.astype(BF16)

    z_arrival(1).wait_recv()
    z_arrival(nt - 1).wait_recv()

    fetches[8].wait()
    near_rows = 5 * rows

    def b_copy(k, h):
        part = pl.ds(h * near_rows, near_rows if h == 0 else all_rows - near_rows)
        return pltpu.make_async_remote_copy(
            src_ref=btx.at[k, part], dst_ref=brx.at[k, part], send_sem=b_send.at[h, k],
            recv_sem=b_recv.at[h, k], device_id=x_dev(k), device_id_type=MESH)

    def project(h):
        part = slice(0, near_rows) if h == 0 else slice(near_rows, all_rows)
        x = xg[part, :]
        for k in range(1, na):
            at = pl.ds(pl.multiple_of(lax.rem(a + k, na) * cols, cols), cols)
            btx[k, part, :] = dot(x, w_ref[:, at]).astype(BF16)
            b_copy(k, h).start()
        acc[part, :] = dot(x, w_ref[:, pl.ds(pl.multiple_of(a * cols, cols), cols)])
    project(0)
    for k in (3, nt - 3, halfway):
        z_arrival(k).wait_recv()
    pk[:, :feat] = dot(route, xg[...]).astype(BF16)

    def y_copy(m):
        return pltpu.make_async_remote_copy(
            src_ref=pk.at[pl.ds(pl.multiple_of(owner_at(m) * spots, spots), spots)],
            dst_ref=rx.at[pl.ds(m * spots, spots)], send_sem=y_send.at[m],
            recv_sem=y_recv.at[m], device_id=(server_at(m), t, a), device_id_type=MESH)

    own = [m for m in range(nd) if m % 2 == 0 and abs(away(m)) < 2]
    others = [m for m in range(nd) if m not in own]
    for m in others:
        y_copy(m).start()
    for k in near_z[early:]:
        u_copy(k).start()

    for m in own:
        rx[m * spots : (m + 1) * spots, :] = pk[pl.ds(pl.multiple_of(owner_at(m) * spots, spots), spots), :]

    def f_copy(m):
        return pltpu.make_async_remote_copy(
            src_ref=ret_tx.at[m], dst_ref=ret_rx.at[m], send_sem=f_send.at[m],
            recv_sem=f_recv.at[m], device_id=(served_at(m), t, a), device_id_type=MESH)

    def swapped(v):
        return jnp.concatenate([v[:, half:], v[:, :half]], axis=1)

    def packed(run):
        lo, hi = run
        return pl.ds(lo * spots // 2, (hi - lo) * spots // 2)

    def p_copy(c, k):
        return pltpu.make_async_remote_copy(
            src_ref=ptx.at[packed(runs[c])], dst_ref=prx.at[k, packed(runs[c])], send_sem=p_send.at[c, k],
            recv_sem=p_recv.at[c, k], device_id=x_dev(k), device_id_type=MESH)

    def r_copy(c, k, block):
        part = redg.at[block, packed(runs[c])]
        return pltpu.make_async_remote_copy(
            src_ref=part, dst_ref=part, send_sem=r_send.at[c, k],
            recv_sem=r_recv.at[c, k], device_id=z_dev(k), device_id_type=MESH)

    def down_of(c):
        lo, hi = runs[c]
        n = (hi - lo) * spots
        for m in range(lo, hi):
            if m in others:
                y_copy(m).wait_recv()
        shrunk = jnp.concatenate(
            [dot_t(rx[first * spots : last * spots, :feat], downp[side]) for first, last, side in maps_of(lo, hi)], axis=0)
        at = iota((n, lanes), 1)
        held = rx[lo * spots : hi * spots, feat + 1 : feat + 2].astype(F32)
        shrunk = jnp.where((at // half).astype(F32) == held, shrunk, 0.0)
        shrunk = shrunk + swapped(shrunk)
        shrunk = jnp.where(at[: n // 2] < half, shrunk[: n // 2], shrunk[n // 2 :])
        ptx[packed(runs[c]), :] = shrunk.astype(BF16)
        for k in range(1, na):
            p_copy(c, k).start()
        return shrunk

    def sum_of(c, shrunk):
        for k in range(1, na):
            p_copy(c, k).wait_recv()
            shrunk = shrunk + prx[k, packed(runs[c]), :].astype(F32)
        redg[t, packed(runs[c]), :] = shrunk.astype(BF16)

        def r_start(k, s):
            r_copy(c, k, t).start()
            return s
        lax.fori_loop(1, nt, r_start, 0)

    def up_of(c):
        lo, hi = runs[c]
        n = (hi - lo) * spots

        def r_wait(k, s):
            r_copy(c, k, lax.rem(t - k + nt, nt)).wait_recv()
            return s
        lax.fori_loop(1, nt, r_wait, 0)
        if c == 0:
            def v_wait(k, s):
                for side in (1, 2):
                    v_copy(side, k).wait_recv()
                return s
            lax.fori_loop(0, nt, v_wait, 0)
        at = iota((n, lanes), 1)
        low = at[: n // 2] < half
        for g in range(nt):
            both = redg[g, packed(runs[c]), :].astype(F32)
            turned = swapped(both)
            spread = jnp.concatenate([jnp.where(low, both, turned), jnp.where(low, turned, both)], axis=0)
            held = rx[lo * spots : hi * spots, feat + 8 + g : feat + 9 + g].astype(F32) - 1.0
            spread = jnp.where((at // half).astype(F32) == held, spread, 0.0).astype(BF16)
            for first, last, side in maps_of(lo, hi):
                grown = dot(spread[(first - lo) * spots : (last - lo) * spots], upg[side, g]).astype(BF16)
                ret_tx[first:last, g, :, :] = grown.reshape(last - first, spots, cols)
        for m in range(lo, hi):
            if m in others:
                f_copy(m).start()

    for side in (1, 2):
        d_copy(side).wait_recv()
    near_sum = down_of(0)
    sum_of(0, near_sum)
    hand_on(early, 4)
    first_sum = down_of(1)
    hand_on(4, 5)
    sum_of(1, first_sum)
    hand_on(5, 6)
    next_sum = down_of(2)
    hand_on(6, nt)
    sum_of(2, next_sum)
    project(1)
    up_of(0)
    up_of(1)
    up_of(2)
    for m in own:
        ret_rx[m] = ret_tx[m]
    for h in (0, 1):
        for k in range(1, na):
            b_copy(k, h).wait_recv()
    for k in range(1, na):
        acc[...] += brx[k].astype(F32)

    target = owners * spots + place
    def drain_z(k, c):
        u_copy(k).wait_send()
        for r in range(len(runs)):
            r_copy(r, k, t).wait_send()
        return c
    lax.fori_loop(1, nt, drain_z, 0)
    for copy in z_first + z_second:
        z_copy(*copy).wait_send()

    def drain_v(k, c):
        for side in (1, 2):
            v_copy(side, k).wait_send()
        return c
    lax.fori_loop(0, nt, drain_v, 0)
    for side in (1, 2):
        d_copy(side).wait_send()
    for k in order_z[1:]:
        t_copy(k).wait_send()
    for m in others:
        y_copy(m).wait_send()
    for k in range(1, na):
        b_copy(k, 0).wait_send()
        b_copy(k, 1).wait_send()
        for c in range(len(runs)):
            p_copy(c, k).wait_send()

    total = acc[...]
    span = nt * spots
    for m in range(nd):
        if m in others:
            f_copy(m).wait_recv()
        place_of = (iota((all_rows, span), 1) + owner_at(m) * span).astype(F32)
        pick = jnp.where(place_of == target, 1.0, 0.0).astype(BF16)
        total = total + dot(pick, ret_rx[m].reshape(span, cols))
    for k in range(nt):
        out_ref[pl.ds(pl.multiple_of(lax.rem(t - k + nt, nt) * rows, rows), rows), :] = total[
            pos_z[k] * rows : (pos_z[k] + 1) * rows].astype(BF16)
    for m in others:
        f_copy(m).wait_send()


def body(sizes, q, kc, vc, lengths, index, table, w, down, up):
    nd, nt, na = sizes
    rows, groups, _, width = q.shape
    cache = kc.shape[1]
    holding, rank = down.shape[0], down.shape[1]
    feat = groups * width
    columns = w.shape[-1]
    cols = columns // na
    spots = nt * CAP
    slots = nd * spots
    wide = feat + holding * rank
    hr = holding * rank
    parts = len(order_of(nd // 2)[1])
    dma = pltpu.SemaphoreType.DMA
    return pl.pallas_call(
        functools.partial(kernel, nd, nt, na, groups, cache, holding),
        out_shape=jax.ShapeDtypeStruct((nt * rows, cols), BF16),
        in_specs=[pl.BlockSpec(memory_space=pltpu.HBM)] * 9,
        out_specs=pl.BlockSpec(memory_space=pltpu.VMEM),
        scratch_shapes=[
            pltpu.VMEM((rows * groups, width), BF16),
            pltpu.VMEM((rows * cache, width), BF16),
            pltpu.VMEM((rows * cache, width), BF16),
            pltpu.VMEM((1, rows), jnp.int32),
            pltpu.VMEM((1, rows), jnp.int32),
            pltpu.VMEM((1, table.shape[0]), jnp.int32),
            pltpu.VMEM((hr * groups, width), BF16),
            pltpu.VMEM((hr * nt, cols), BF16),
            pltpu.VMEM((nt * rows, feat), BF16),
            pltpu.VMEM((nt * rows, hr), BF16),
            pltpu.VMEM((slots, wide), BF16),
            pltpu.VMEM((slots, wide), BF16),
            pltpu.VMEM((feat, columns), BF16),
            pltpu.VMEM((3, hr, feat), BF16),
            pltpu.VMEM((nt, hr, cols), BF16),
            pltpu.VMEM((3, nt, hr, cols), BF16),
            pltpu.VMEM((na, nt * rows, cols), BF16),
            pltpu.VMEM((na, nt * rows, cols), BF16),
            pltpu.VMEM((nt * rows, cols), F32),
            pltpu.VMEM((slots // 2, hr), BF16),
            pltpu.VMEM((na, slots // 2, hr), BF16),
            pltpu.VMEM((nt, slots // 2, hr), BF16),
            pltpu.VMEM((nd, nt, spots, cols), BF16),
            pltpu.VMEM((nd, nt, spots, cols), BF16),
            dma((9,)),
            dma((nt,)), dma((nt,)), dma((nt,)), dma((nt,)),
            dma((nd,)), dma((nd,)),
            dma((2, na)), dma((2, na)), dma((parts, na)), dma((parts, na)),
            dma((parts, nt)), dma((parts, nt)),
            dma((nd,)), dma((nd,)),
            dma((3,)), dma((3,)), dma((3, nt)), dma((3, nt)),
            dma((nt,)), dma((nt,)),
        ],
        compiler_params=pltpu.CompilerParams(
            collective_id=0, has_side_effects=True, vmem_limit_bytes=60 * 1024 * 1024
        ),
    )(
        q.reshape(rows * groups, width),
        kc.reshape(rows * cache, width),
        vc.reshape(rows * cache, width),
        lengths.reshape(1, rows),
        index.reshape(1, rows),
        table.reshape(1, -1),
        w.reshape(feat, columns),
        down.reshape(hr * groups, width),
        up.reshape(hr * nt, cols),
    )


def solution(mesh):
    sizes = tuple(mesh.shape[name] for name in ("dp", "tensor", "adapter"))
    return jax.shard_map(
        functools.partial(body, sizes),
        mesh=mesh,
        in_specs=(
            P(("dp", "tensor"), None, "adapter", None),
            P(("dp", "tensor"), None, "adapter", None),
            P(("dp", "tensor"), None, "adapter", None),
            P(("dp", "tensor")),
            P(("dp", "tensor")),
            P(),
            P(None, "adapter", None, "tensor"),
            P(("dp", "tensor"), None, None, "adapter", None),
            P(("dp", "tensor"), None, None, "adapter"),
        ),
        out_specs=P("dp", ("tensor", "adapter")),
        check_vma=False,
    )
```

```python
import functools

import jax
import jax.numpy as jnp
from jax import lax
from jax.experimental import pallas as pl
from jax.experimental.pallas import tpu as pltpu
from jax.sharding import PartitionSpec as P

MESH = pl.DeviceIdType.MESH
CAP = 2
F32 = jnp.float32
BF16 = jnp.bfloat16


def iota(shape, dim):
    return lax.broadcasted_iota(jnp.int32, shape, dim)


def dot(a, b):
    return jnp.dot(a, b, preferred_element_type=F32)


def dot_t(a, b):
    return lax.dot_general(a, b, (((1,), (1,)), ((), ())), preferred_element_type=F32)


def regroup(rows, groups):
    n = rows * groups
    out, into = iota((n, n), 0), iota((n, n), 1)
    return jnp.where(into == (out % rows) * groups + out // rows, 1.0, 0.0).astype(BF16)


def column_of(row, n):
    return jnp.sum(jnp.where(iota((n, n), 0) == iota((n, n), 1), row, 0.0), axis=1, keepdims=True)


def row_of(column, n):
    return jnp.sum(jnp.where(iota((n, n), 0) == iota((n, n), 1), column, 0.0), axis=0, keepdims=True)


def attend(q_ref, k_ref, v_ref, length_row, rows, groups, cache):
    per = 128 // cache if rows * cache > 128 else rows
    width = per * cache
    lengths = jnp.sum(
        jnp.where(iota((rows * groups, rows), 0) // groups == iota((rows * groups, rows), 1), length_row, 0.0),
        axis=1,
        keepdims=True,
    )
    outs = []
    for first in range(0, rows, per):
        q = q_ref[first * groups : (first + per) * groups, :]
        k = k_ref[first * cache : (first + per) * cache, :]
        v = v_ref[first * cache : (first + per) * cache, :]
        shape = (per * groups, width)
        lane = iota(shape, 1)
        live = (iota(shape, 0) // groups == lane // cache) & (
            (lane % cache).astype(F32) < lengths[first * groups : (first + per) * groups, :]
        )
        scores = jnp.where(live, dot_t(q, k) * (q.shape[-1] ** -0.5), -1e30)
        weights = jnp.exp(scores - jnp.max(scores, axis=1, keepdims=True))
        weights = jnp.where(live, weights, 0.0)
        weights = (weights / jnp.sum(weights, axis=1, keepdims=True)).astype(BF16)
        outs.append(dot(weights, v).astype(BF16))
    return jnp.concatenate(outs, axis=0)


def order_of(chips):
    half = chips // 2
    near = [0, 1, -1, 2, -2] + list(range(3, half + 1)) + [-j for j in range(3, half)]
    return near, [(0, 6), (6, 10), (10, 2 * chips)]


def ring_order(n):
    return sorted(range(n), key=lambda k: min(k, n - k))


def sign(j):
    return (j > 0) - (j < 0)


def kernel(
    nd, nt, na, groups, cache, holding,
    q_hbm, k_hbm, v_hbm, len_hbm, idx_hbm, slot_hbm, w_hbm, down_hbm, up_hbm, out_ref,
    q_ref, k_ref, v_ref, len_ref, idx_ref, slot_ref, down_ref, up_ref,
    xg, tg, pk, rx, w_ref, downp, upp, upg, btx, brx, acc, ptx, prx, redg, ret_tx, ret_rx,
    in_sem, z_send, z_recv, u_send, u_recv, y_send, y_recv, b_send, b_recv, p_send, p_recv,
    r_send, r_recv, f_send, f_recv, d_send, d_recv, v_send, v_recv, t_send, t_recv,
):
    d, t, a = lax.axis_index("dp"), lax.axis_index("tensor"), lax.axis_index("adapter")
    rows = q_ref.shape[0] // groups
    feat = groups * 128
    spots = nt * CAP
    slots = nd * spots
    half = 64
    lanes = 2 * half
    all_rows = nt * rows
    cols = acc.shape[1]
    chips = nd // 2
    near, runs = order_of(chips)
    chip, core = d // 2, d % 2

    def away(m):
        j = near[m // 2]
        return -j if 2 * j == chips and m % 2 else j

    def at_chip(j, m):
        return 2 * lax.rem(chip + j + chips, chips) + lax.rem(core + m % 2, 2)

    def owner_at(m):
        return at_chip(away(m), m)

    def server_at(m):
        return at_chip(away(m) - sign(away(m)), m)

    def served_at(m):
        return at_chip(sign(away(m)) - away(m), m)

    def maps_of(lo, hi):
        found = []
        for m in range(lo, hi):
            side = (0, 1, 2)[sign(away(m))]
            if found and found[-1][2] == side:
                found[-1][1] = m + 1
            else:
                found.append([m, m + 1, side])
        return found

    def z_dev(k):
        return (d, lax.rem(t + k, nt), a)

    def x_dev(k):
        return (d, t, lax.rem(a + k, na))

    fetches = [
        pltpu.make_async_copy(src, dst, in_sem.at[n])
        for n, (src, dst) in enumerate((
            (q_hbm, q_ref), (k_hbm, k_ref), (len_hbm, len_ref), (v_hbm, v_ref), (idx_hbm, idx_ref),
            (slot_hbm, slot_ref), (up_hbm, up_ref), (down_hbm, down_ref), (w_hbm, w_ref)))
    ]
    for fetch in fetches:
        fetch.start()
    barrier = pltpu.get_barrier_semaphore()

    def greet_z(k, c):
        pl.semaphore_signal(barrier, inc=1, device_id=z_dev(k), device_id_type=MESH)
        return c

    def greet_y(k, c):
        pl.semaphore_signal(barrier, inc=1, device_id=(lax.rem(d + k, nd), t, a), device_id_type=MESH)
        return c

    def greet_x(k, c):
        pl.semaphore_signal(barrier, inc=1, device_id=x_dev(k), device_id_type=MESH)
        return c
    lax.fori_loop(1, nt, greet_z, 0)
    lax.fori_loop(1, nd, greet_y, 0)
    lax.fori_loop(1, na, greet_x, 0)

    for fetch in fetches[:4]:
        fetch.wait()
    att = attend(q_ref, k_ref, v_ref, len_ref[...].astype(F32), rows, groups, cache)
    swap = regroup(rows, groups)
    att = dot(swap, att).astype(BF16)
    for g in range(groups):
        xg[0:rows, g * 128 : (g + 1) * 128] = att[g * rows : (g + 1) * rows, :]

    pl.semaphore_wait(barrier, (nt - 1) + (nd - 1) + (na - 1))
    order_z = ring_order(nt)
    pos_z = [order_z.index(k) for k in range(nt)]

    def z_part(place):
        return xg.at[pl.ds(place * rows, rows)]

    def z_copy(place, hop, far):
        return pltpu.make_async_remote_copy(
            src_ref=z_part(place), dst_ref=z_part(pos_z[far]), send_sem=z_send.at[far], recv_sem=z_recv.at[far],
            device_id=(d, lax.rem(t + hop + nt, nt), a), device_id_type=MESH)

    def z_arrival(k):
        return pltpu.make_async_remote_copy(
            src_ref=z_part(0), dst_ref=z_part(pos_z[k]), send_sem=z_send.at[k], recv_sem=z_recv.at[k],
            device_id=z_dev(k), device_id_type=MESH)

    halfway = nt // 2
    z_first = [(0, 2, 2), (0, -2, nt - 2), (0, 1, 1), (0, -1, nt - 1)]
    z_second = [
        (pos_z[2], 1, 3), (pos_z[nt - 2], -1, nt - 3),
        (pos_z[2] + (pos_z[nt - 2] - pos_z[2]) * core, 2 - 4 * core, halfway)]
    for copy in z_first:
        z_copy(*copy).start()

    for fetch in fetches[4:6]:
        fetch.wait()
    idx_col = column_of(idx_ref[...].astype(F32), rows)
    table = slot_ref.shape[1]
    slot_col = jnp.sum(
        jnp.where(idx_col == iota((rows, table), 1).astype(F32), slot_ref[...].astype(F32), 0.0),
        axis=1, keepdims=True,
    )
    owner_col = jnp.floor(slot_col * (1.0 / holding))
    local_col = slot_col - holding * owner_col
    owner_row = row_of(owner_col, rows)
    earlier = (owner_row == owner_col) & (iota((rows, rows), 1) < iota((rows, rows), 0))
    pos_col = jnp.sum(jnp.where(earlier, 1.0, 0.0), axis=1, keepdims=True)
    lane = iota((rows, lanes), 1)
    tags = jnp.where(lane == 0, owner_col * CAP + pos_col, jnp.where(lane == 1, local_col, 0.0))

    tg[0:rows, :] = tags.astype(BF16)

    def t_copy(k):
        return pltpu.make_async_remote_copy(
            src_ref=tg.at[pl.ds(0, rows)], dst_ref=tg.at[pl.ds(pos_z[k] * rows, rows)], send_sem=t_send.at[k],
            recv_sem=t_recv.at[k], device_id=z_dev(k), device_id_type=MESH)
    for k in reversed(order_z[1:]):
        t_copy(k).start()

    fetches[6].wait()
    step = 256 // groups
    swap_w = regroup(step, groups)
    for b in range(holding * half // step):
        part = slice(b * step * groups, (b + 1) * step * groups)
        up = dot(swap_w, up_ref[part, :]).astype(BF16)
        for g in range(nt):
            upp[g, b * step : (b + 1) * step, :] = up[g * step : (g + 1) * step, :]
    upg[0, t] = upp[t]

    def u_copy(k):
        return pltpu.make_async_remote_copy(
            src_ref=upp.at[lax.rem(t + k, nt)], dst_ref=upg.at[0, t], send_sem=u_send.at[k],
            recv_sem=u_recv.at[k], device_id=z_dev(k), device_id_type=MESH)

    def u_arrival(k):
        return pltpu.make_async_remote_copy(
            src_ref=upp.at[lax.rem(t + k, nt)], dst_ref=upg.at[0, lax.rem(t - k + nt, nt)], send_sem=u_send.at[k],
            recv_sem=u_recv.at[k], device_id=z_dev(k), device_id_type=MESH)

    def beside_dev(side):
        return (at_chip(1 if side == 1 else -1, 0), t, a)

    def d_copy(side):
        return pltpu.make_async_remote_copy(
            src_ref=downp.at[0], dst_ref=downp.at[3 - side], send_sem=d_send.at[side],
            recv_sem=d_recv.at[3 - side], device_id=beside_dev(side), device_id_type=MESH)

    def v_copy(side, k):
        block = lax.rem(t - k + nt, nt)
        return pltpu.make_async_remote_copy(
            src_ref=upg.at[0, block], dst_ref=upg.at[3 - side, block], send_sem=v_send.at[side, k],
            recv_sem=v_recv.at[3 - side, k], device_id=beside_dev(side), device_id_type=MESH)

    for side in (1, 2):
        v_copy(side, 0).start()
    near_z = ring_order(nt)[1:]
    early = 2
    for k in near_z[:early]:
        u_copy(k).start()

    def hand_on(first, last):
        for k in near_z[first:last]:
            u_arrival(k).wait_recv()
            for side in (1, 2):
                v_copy(side, k).start()

    fetches[7].wait()
    for b in range(holding * half // step):
        part = slice(b * step * groups, (b + 1) * step * groups)
        down = dot(swap_w, down_ref[part, :]).astype(BF16)
        for g in range(groups):
            downp[0, b * step : (b + 1) * step, g * 128 : (g + 1) * 128] = down[g * step : (g + 1) * step, :]
    for side in (1, 2):
        d_copy(side).start()

    z_arrival(2).wait_recv()
    z_copy(*z_second[0]).start()
    z_arrival(nt - 2).wait_recv()
    z_copy(*z_second[1]).start()
    z_copy(*z_second[2]).start()
    hand_on(0, early)
    for k in order_z[1:]:
        t_copy(k).wait_recv()
    tag = tg[...].astype(F32)
    codes, local = tag[:, 0:1], tag[:, 1:2]
    owners = jnp.floor(codes * (1.0 / CAP))
    pos = codes - CAP * owners
    owner_d = jnp.floor(owners * (1.0 / nt))
    owner_t = owners - nt * owner_d
    block = iota((all_rows, 1), 0) // rows
    block = jnp.where(block % 2 == 1, (block + 1) // 2, nt - block // 2)
    place = ((t - block + nt) % nt).astype(F32) * CAP + pos
    target = owner_d * spots + place
    target_row = row_of(target, all_rows)
    here_row = row_of(jnp.where(owner_t == t.astype(F32), 1.0, 0.0), all_rows)
    route = jnp.where(iota((slots, all_rows), 0).astype(F32) == target_row, 1.0, 0.0)
    wide_lane = iota((all_rows, lanes), 1)
    places = jnp.where((wide_lane - 8).astype(F32) == owner_t, local + 1.0, 0.0).astype(BF16)
    beside = dot(route.astype(BF16), places)
    route = (route * here_row).astype(BF16)
    beside = beside + jnp.where(iota((slots, lanes), 1) == 1, dot(route, tg[...]), 0.0)
    pk[:, feat : feat + lanes] = beside.astype(BF16)

    z_arrival(1).wait_recv()
    z_arrival(nt - 1).wait_recv()

    fetches[8].wait()
    near_rows = 5 * rows

    def b_copy(k, h):
        part = pl.ds(h * near_rows, near_rows if h == 0 else all_rows - near_rows)
        return pltpu.make_async_remote_copy(
            src_ref=btx.at[k, part], dst_ref=brx.at[k, part], send_sem=b_send.at[h, k],
            recv_sem=b_recv.at[h, k], device_id=x_dev(k), device_id_type=MESH)

    def project(h):
        part = slice(0, near_rows) if h == 0 else slice(near_rows, all_rows)
        x = xg[part, :]
        for k in range(1, na):
            at = pl.ds(pl.multiple_of(lax.rem(a + k, na) * cols, cols), cols)
            btx[k, part, :] = dot(x, w_ref[:, at]).astype(BF16)
            b_copy(k, h).start()
        acc[part, :] = dot(x, w_ref[:, pl.ds(pl.multiple_of(a * cols, cols), cols)])
    project(0)
    for k in (3, nt - 3, halfway):
        z_arrival(k).wait_recv()
    pk[:, :feat] = dot(route, xg[...]).astype(BF16)

    def y_copy(m):
        return pltpu.make_async_remote_copy(
            src_ref=pk.at[pl.ds(pl.multiple_of(owner_at(m) * spots, spots), spots)],
            dst_ref=rx.at[pl.ds(m * spots, spots)], send_sem=y_send.at[m],
            recv_sem=y_recv.at[m], device_id=(server_at(m), t, a), device_id_type=MESH)

    own = [m for m in range(nd) if m % 2 == 0 and abs(away(m)) < 2]
    others = [m for m in range(nd) if m not in own]
    for m in others:
        y_copy(m).start()
    for k in near_z[early:]:
        u_copy(k).start()

    for m in own:
        rx[m * spots : (m + 1) * spots, :] = pk[pl.ds(pl.multiple_of(owner_at(m) * spots, spots), spots), :]

    def f_copy(m):
        return pltpu.make_async_remote_copy(
            src_ref=ret_tx.at[m], dst_ref=ret_rx.at[m], send_sem=f_send.at[m],
            recv_sem=f_recv.at[m], device_id=(served_at(m), t, a), device_id_type=MESH)

    def swapped(v):
        return jnp.concatenate([v[:, half:], v[:, :half]], axis=1)

    def packed(run):
        lo, hi = run
        return pl.ds(lo * spots // 2, (hi - lo) * spots // 2)

    def p_copy(c, k):
        return pltpu.make_async_remote_copy(
            src_ref=ptx.at[packed(runs[c])], dst_ref=prx.at[k, packed(runs[c])], send_sem=p_send.at[c, k],
            recv_sem=p_recv.at[c, k], device_id=x_dev(k), device_id_type=MESH)

    def r_copy(c, k, block):
        part = redg.at[block, packed(runs[c])]
        return pltpu.make_async_remote_copy(
            src_ref=part, dst_ref=part, send_sem=r_send.at[c, k],
            recv_sem=r_recv.at[c, k], device_id=z_dev(k), device_id_type=MESH)

    def down_of(c):
        lo, hi = runs[c]
        n = (hi - lo) * spots
        for m in range(lo, hi):
            if m in others:
                y_copy(m).wait_recv()
        shrunk = jnp.concatenate(
            [dot_t(rx[first * spots : last * spots, :feat], downp[side]) for first, last, side in maps_of(lo, hi)], axis=0)
        at = iota((n, lanes), 1)
        held = rx[lo * spots : hi * spots, feat + 1 : feat + 2].astype(F32)
        shrunk = jnp.where((at // half).astype(F32) == held, shrunk, 0.0)
        shrunk = shrunk + swapped(shrunk)
        shrunk = jnp.where(at[: n // 2] < half, shrunk[: n // 2], shrunk[n // 2 :])
        ptx[packed(runs[c]), :] = shrunk.astype(BF16)
        for k in range(1, na):
            p_copy(c, k).start()
        return shrunk

    def sum_of(c, shrunk):
        for k in range(1, na):
            p_copy(c, k).wait_recv()
            shrunk = shrunk + prx[k, packed(runs[c]), :].astype(F32)
        redg[t, packed(runs[c]), :] = shrunk.astype(BF16)

        for k in reversed(order_z[1:]):
            r_copy(c, k, t).start()

    def up_of(c):
        lo, hi = runs[c]
        n = (hi - lo) * spots

        def r_wait(k, s):
            r_copy(c, k, lax.rem(t - k + nt, nt)).wait_recv()
            return s
        lax.fori_loop(1, nt, r_wait, 0)
        if c == 0:
            def v_wait(k, s):
                for side in (1, 2):
                    v_copy(side, k).wait_recv()
                return s
            lax.fori_loop(0, nt, v_wait, 0)
        at = iota((n, lanes), 1)
        low = at[: n // 2] < half
        for g in range(nt):
            both = redg[g, packed(runs[c]), :].astype(F32)
            turned = swapped(both)
            spread = jnp.concatenate([jnp.where(low, both, turned), jnp.where(low, turned, both)], axis=0)
            held = rx[lo * spots : hi * spots, feat + 8 + g : feat + 9 + g].astype(F32) - 1.0
            spread = jnp.where((at // half).astype(F32) == held, spread, 0.0).astype(BF16)
            for first, last, side in maps_of(lo, hi):
                grown = dot(spread[(first - lo) * spots : (last - lo) * spots], upg[side, g]).astype(BF16)
                ret_tx[first:last, g, :, :] = grown.reshape(last - first, spots, cols)
        for m in range(lo, hi):
            if m in others:
                f_copy(m).start()

    for side in (1, 2):
        d_copy(side).wait_recv()
    near_sum = down_of(0)
    hand_on(early, 4)
    sum_of(0, near_sum)
    first_sum = down_of(1)
    hand_on(4, 5)
    sum_of(1, first_sum)
    hand_on(5, 6)
    next_sum = down_of(2)
    hand_on(6, nt)
    sum_of(2, next_sum)
    project(1)
    up_of(0)
    up_of(1)
    up_of(2)
    for m in own:
        ret_rx[m] = ret_tx[m]
    for h in (0, 1):
        for k in range(1, na):
            b_copy(k, h).wait_recv()
    for k in range(1, na):
        acc[...] += brx[k].astype(F32)

    target = owners * spots + place
    def drain_z(k, c):
        u_copy(k).wait_send()
        for r in range(len(runs)):
            r_copy(r, k, t).wait_send()
        return c
    lax.fori_loop(1, nt, drain_z, 0)
    for copy in z_first + z_second:
        z_copy(*copy).wait_send()

    def drain_v(k, c):
        for side in (1, 2):
            v_copy(side, k).wait_send()
        return c
    lax.fori_loop(0, nt, drain_v, 0)
    for side in (1, 2):
        d_copy(side).wait_send()
    for k in order_z[1:]:
        t_copy(k).wait_send()
    for m in others:
        y_copy(m).wait_send()
    for k in range(1, na):
        b_copy(k, 0).wait_send()
        b_copy(k, 1).wait_send()
        for c in range(len(runs)):
            p_copy(c, k).wait_send()

    total = acc[...]
    span = nt * spots
    for m in range(nd):
        if m in others:
            f_copy(m).wait_recv()
        place_of = (iota((all_rows, span), 1) + owner_at(m) * span).astype(F32)
        pick = jnp.where(place_of == target, 1.0, 0.0).astype(BF16)
        total = total + dot(pick, ret_rx[m].reshape(span, cols))
    for k in range(nt):
        out_ref[pl.ds(pl.multiple_of(lax.rem(t - k + nt, nt) * rows, rows), rows), :] = total[
            pos_z[k] * rows : (pos_z[k] + 1) * rows].astype(BF16)
    for m in others:
        f_copy(m).wait_send()


def body(sizes, q, kc, vc, lengths, index, table, w, down, up):
    nd, nt, na = sizes
    rows, groups, _, width = q.shape
    cache = kc.shape[1]
    holding, rank = down.shape[0], down.shape[1]
    feat = groups * width
    columns = w.shape[-1]
    cols = columns // na
    spots = nt * CAP
    slots = nd * spots
    wide = feat + holding * rank
    hr = holding * rank
    parts = len(order_of(nd // 2)[1])
    dma = pltpu.SemaphoreType.DMA
    return pl.pallas_call(
        functools.partial(kernel, nd, nt, na, groups, cache, holding),
        out_shape=jax.ShapeDtypeStruct((nt * rows, cols), BF16),
        in_specs=[pl.BlockSpec(memory_space=pltpu.HBM)] * 9,
        out_specs=pl.BlockSpec(memory_space=pltpu.VMEM),
        scratch_shapes=[
            pltpu.VMEM((rows * groups, width), BF16),
            pltpu.VMEM((rows * cache, width), BF16),
            pltpu.VMEM((rows * cache, width), BF16),
            pltpu.VMEM((1, rows), jnp.int32),
            pltpu.VMEM((1, rows), jnp.int32),
            pltpu.VMEM((1, table.shape[0]), jnp.int32),
            pltpu.VMEM((hr * groups, width), BF16),
            pltpu.VMEM((hr * nt, cols), BF16),
            pltpu.VMEM((nt * rows, feat), BF16),
            pltpu.VMEM((nt * rows, hr), BF16),
            pltpu.VMEM((slots, wide), BF16),
            pltpu.VMEM((slots, wide), BF16),
            pltpu.VMEM((feat, columns), BF16),
            pltpu.VMEM((3, hr, feat), BF16),
            pltpu.VMEM((nt, hr, cols), BF16),
            pltpu.VMEM((3, nt, hr, cols), BF16),
            pltpu.VMEM((na, nt * rows, cols), BF16),
            pltpu.VMEM((na, nt * rows, cols), BF16),
            pltpu.VMEM((nt * rows, cols), F32),
            pltpu.VMEM((slots // 2, hr), BF16),
            pltpu.VMEM((na, slots // 2, hr), BF16),
            pltpu.VMEM((nt, slots // 2, hr), BF16),
            pltpu.VMEM((nd, nt, spots, cols), BF16),
            pltpu.VMEM((nd, nt, spots, cols), BF16),
            dma((9,)),
            dma((nt,)), dma((nt,)), dma((nt,)), dma((nt,)),
            dma((nd,)), dma((nd,)),
            dma((2, na)), dma((2, na)), dma((parts, na)), dma((parts, na)),
            dma((parts, nt)), dma((parts, nt)),
            dma((nd,)), dma((nd,)),
            dma((3,)), dma((3,)), dma((3, nt)), dma((3, nt)),
            dma((nt,)), dma((nt,)),
        ],
        compiler_params=pltpu.CompilerParams(
            collective_id=0, has_side_effects=True, vmem_limit_bytes=60 * 1024 * 1024
        ),
    )(
        q.reshape(rows * groups, width),
        kc.reshape(rows * cache, width),
        vc.reshape(rows * cache, width),
        lengths.reshape(1, rows),
        index.reshape(1, rows),
        table.reshape(1, -1),
        w.reshape(feat, columns),
        down.reshape(hr * groups, width),
        up.reshape(hr * nt, cols),
    )


def solution(mesh):
    sizes = tuple(mesh.shape[name] for name in ("dp", "tensor", "adapter"))
    return jax.shard_map(
        functools.partial(body, sizes),
        mesh=mesh,
        in_specs=(
            P(("dp", "tensor"), None, "adapter", None),
            P(("dp", "tensor"), None, "adapter", None),
            P(("dp", "tensor"), None, "adapter", None),
            P(("dp", "tensor")),
            P(("dp", "tensor")),
            P(),
            P(None, "adapter", None, "tensor"),
            P(("dp", "tensor"), None, None, "adapter", None),
            P(("dp", "tensor"), None, None, "adapter"),
        ),
        out_specs=P("dp", ("tensor", "adapter")),
        check_vma=False,
    )
```
